512 devices in a mesh: dp: 32 (over x_lo, z), blk: 16 (over y, x_hi, core).
Axes of the slice: x: 4 (x_hi: 2, x_lo: 2; x = x_hi * 2 + x_lo), y: 4, z: 16, core: 2. Of those that a mesh axis runs over, the one named last changes fastest.
Arguments:
- tokens: bfloat16 [131072, 1024], P(('dp', 'blk')), may hold values from -6 to 6
- lengths: int32 [4096], P(('dp', 'blk')), may hold values from 1 to 32
- cotangent: bfloat16 [131072, 1024], P(('dp', 'blk')), may hold values from -6 to 6
- input_weight: bfloat16 [1024, 1536], P('blk'), may hold values from -0.1875 to 0.1875
- output_weight: bfloat16 [1024, 512], P('blk'), may hold values from -0.25 to 0.25
Outputs:
- layer_out: bfloat16 [131072, 1024], P(('dp', 'blk'))
- grad_tokens: bfloat16 [131072, 1024], P(('dp', 'blk'))
- grad_input_weight: float32 [1024, 1536], P('blk')
- grad_output_weight: float32 [1024, 512], P('blk')
The draws below stay inside these ranges and needn't reach their ends.
Inputs may be any that keep to these rules, and one draw needn't show every extreme that they name: `lengths`: number of real tokens of each caption; tokens past it are padding.
All inputs are finite; a program needn't handle non-finite values.
Results may differ from the reference program's by a relative error of at most 0.035.
Values may be sent and summed in bfloat16 or wider, within the bound.
A program may use at most 64 MiB of HBM per device.

```python
import jax
import jax.numpy as jnp
from jax import lax

D = 1024
HEADS = 8
HEAD_SIZE = 64
CAPLEN = 32
TOK_DEV = 256
CAPTIONS = 4096
TOKENS = 131072
DEVICES = 512


def with_ends(array, stream_key, smallest, largest):
    longest = array.shape.index(max(array.shape))
    spots = []
    for shift in (0, 1):
        where = [jax.random.randint(jax.random.fold_in(stream_key, axis), (), 0, length) for axis, length in enumerate(array.shape)]
        where[longest] = (where[longest] + shift) % array.shape[longest]
        spots.append(tuple(where))
    return array.at[spots[0]].set(smallest).at[spots[1]].set(largest)


def block_scale(rng, dims, split, smallest, largest):
    gain, own = 1.0, jax.random.fold_in(rng, 6)
    for axis_at, shards_of in split:
        draws = jnp.exp(jax.random.uniform(jax.random.fold_in(own, axis_at), (shards_of,), jnp.float32, smallest / len(split), largest / len(split)))
        gain = gain * jnp.repeat(draws, dims[axis_at] // shards_of).reshape([-1 if axis == axis_at else 1 for axis in range(len(dims))])
    return gain


def gaussian(stream_key, dims, scale, most, split=(), held_as=jnp.bfloat16):
    result = jax.random.normal(stream_key, dims, jnp.float32) * scale
    if len(split) > 0:
        result = block_scale(stream_key, dims, split, -0.22, 0.18) * result
    return jnp.clip(result, min=-most, max=most).astype(held_as)


def setup_inputs(seed: int = 0) -> dict:
    keys = jax.random.split(jax.random.key(seed), 6)
    return {
        "tokens": gaussian(keys[0], (TOKENS, D), 1.0, 6.0, ((0, 512),)),
        "lengths": with_ends(jax.random.randint(keys[1], (CAPTIONS,), 1, CAPLEN + 1), jax.random.fold_in(keys[1], 1), 1, CAPLEN).astype(jnp.int32),
        "cotangent": gaussian(keys[2], (TOKENS, D), 1.0, 6.0, ((0, 512),)),
        "input_weight": gaussian(keys[3], (D, 3 * HEADS * HEAD_SIZE), D ** -0.5, 0.1875, ((0, 16),)),
        "output_weight": gaussian(keys[4], (D, HEADS * HEAD_SIZE), (HEADS * HEAD_SIZE) ** -0.5, 0.25, ((0, 16),)),
    }


EPSILON = 1e-06

def attend_block(projected, lengths):
    head_dim = HEADS * HEAD_SIZE
    captions = projected.shape[0] // CAPLEN
    score_scale = HEAD_SIZE ** (-0.5)
    query_rows = projected[:, :head_dim].reshape(captions, CAPLEN, HEADS, HEAD_SIZE).astype(jnp.float32)
    key_rows = projected[:, head_dim:2 * head_dim].reshape(captions, CAPLEN, HEADS, HEAD_SIZE).astype(jnp.float32)
    value_rows = projected[:, 2 * head_dim:].reshape(captions, CAPLEN, HEADS, HEAD_SIZE).astype(jnp.float32)
    scores = jnp.einsum('clhe,cmhe->chlm', query_rows, key_rows) * score_scale
    position = jnp.arange(CAPLEN, dtype=jnp.int32)
    causal = position[None, :] <= position[:, None]
    allowed = causal[None, :, :] & (position[None, None, :] < lengths.astype(jnp.int32)[:, None, None])
    raised = jnp.where(allowed[:, None, :, :], jnp.exp(scores), jnp.float32(0.0))
    probability = raised / lax.optimization_barrier(jnp.sum(raised, axis=-1, keepdims=True))
    rounded_prob = probability.astype(jnp.bfloat16)
    attended = jnp.einsum('chlm,cmhe->clhe', rounded_prob.astype(jnp.float32), value_rows)
    attended = attended.reshape(projected.shape[0], head_dim).astype(jnp.bfloat16)
    return (attended, probability, rounded_prob, query_rows, key_rows, value_rows)

def layer_block(tokens, lengths, cotangent, input_weight, output_weight):
    head_dim = HEADS * HEAD_SIZE
    row_count = tokens.shape[0]
    captions = row_count // CAPLEN
    score_scale = HEAD_SIZE ** (-0.5)
    floats = tokens.astype(jnp.float32)
    inverse = lax.rsqrt(lax.optimization_barrier(jnp.mean(floats * floats, axis=-1, keepdims=True)) + EPSILON)
    normed = (floats * inverse).astype(jnp.bfloat16)
    projected = jnp.dot(normed, input_weight, preferred_element_type=jnp.float32).astype(jnp.bfloat16)
    attended, probability, rounded_prob, query_rows, key_rows, value_rows = attend_block(projected, lengths)
    mixed = lax.dot_general(attended, output_weight, (((1,), (1,)), ((), ())), preferred_element_type=jnp.float32)
    layer_out = (floats + mixed).astype(jnp.bfloat16)
    grad_attended = jnp.dot(cotangent, output_weight, preferred_element_type=jnp.float32).astype(jnp.bfloat16)
    grad_heads = grad_attended.reshape(captions, CAPLEN, HEADS, HEAD_SIZE).astype(jnp.float32)
    grad_prob = jnp.einsum('clhe,cmhe->chlm', grad_heads, value_rows)
    grad_values = jnp.einsum('chlm,clhe->cmhe', rounded_prob.astype(jnp.float32), grad_heads)
    grad_scores = probability * (grad_prob - lax.optimization_barrier(jnp.sum(probability * grad_prob, axis=-1, keepdims=True))) * score_scale
    grad_queries = jnp.einsum('chlm,cmhe->clhe', grad_scores, key_rows)
    grad_keys = jnp.einsum('chlm,clhe->cmhe', grad_scores, query_rows)
    grad_projected = jnp.concatenate([grad_queries.reshape(row_count, head_dim), grad_keys.reshape(row_count, head_dim), grad_values.reshape(row_count, head_dim)], axis=1).astype(jnp.bfloat16)
    grad_normed = lax.dot_general(grad_projected, input_weight, (((1,), (1,)), ((), ())), preferred_element_type=jnp.float32)
    grad_tokens = cotangent.astype(jnp.float32) + inverse * grad_normed - floats * inverse ** 3 * lax.optimization_barrier(jnp.mean(grad_normed * floats, axis=-1, keepdims=True))
    term_project = lax.dot_general(normed, grad_projected, (((0,), (0,)), ((), ())), preferred_element_type=jnp.float32)
    term_output = lax.dot_general(cotangent, attended, (((0,), (0,)), ((), ())), preferred_element_type=jnp.float32)
    return (layer_out, grad_tokens.astype(jnp.bfloat16), term_project, term_output)

def reference(tokens, lengths, cotangent, input_weight, output_weight):
    captions = TOK_DEV // CAPLEN
    token_blocks = tokens.reshape(DEVICES, TOK_DEV, D)
    length_blocks = lengths.reshape(DEVICES, captions)
    cotangent_blocks = cotangent.reshape(DEVICES, TOK_DEV, D)

    def device_step(running, block_item):
        block_tokens, block_lengths, block_cotangent = block_item
        layer_out, grad_tokens, term_project, term_output = layer_block(block_tokens, block_lengths, block_cotangent, input_weight, output_weight)
        rounded_project = lax.optimization_barrier(term_project.astype(jnp.bfloat16)).astype(jnp.float32)
        rounded_output = lax.optimization_barrier(term_output.astype(jnp.bfloat16)).astype(jnp.float32)
        return ((running[0] + rounded_project, running[1] + rounded_output), (layer_out, grad_tokens))
    start_sums = (jnp.zeros(input_weight.shape, jnp.float32), jnp.zeros(output_weight.shape, jnp.float32))
    sums, outputs = lax.scan(device_step, start_sums, (token_blocks, length_blocks, cotangent_blocks))
    layer_out = outputs[0].reshape(TOKENS, D)
    grad_tokens = outputs[1].reshape(TOKENS, D)
    return (layer_out, grad_tokens, sums[0], sums[1])
```

```python
import functools

import jax
import jax.numpy as jnp
from jax import lax
from jax.experimental import pallas as pl
from jax.experimental.pallas import tpu as pltpu
from jax.sharding import PartitionSpec as P

HEADS = 8
HEAD_SIZE = 64
CAPLEN = 32
EPSILON = 1e-06

MESH = pl.DeviceIdType.MESH
NX, NY, NZ = 4, 4, 16
ROWS = 256
D = 1024
HALF = 256
TILE = 128
BF = jnp.bfloat16
F32 = jnp.float32

GATHER = [(cross, dy, dc) for cross in (0, 1) for dy in range(4) for dc in range(2) if cross or dy or dc]
PLANE = [(dx, dy) for dx in range(4) for dy in range(4) if dx or dy]


def device(x, y, z, c):
    return {"dp": (x % 2) * NZ + z, "blk": y * 4 + (x // 2) * 2 + c}


def dot(a, b, ca, cb):
    return lax.dot_general(a, b, (((ca,), (cb,)), ((), ())), preferred_element_type=F32)


def kernel(
    tok_ref, cot_ref, valid_ref, win_ref, wout_ref,
    lo_ref, gt_ref, gin_ref, gout_ref,
    stage, w, tok2, cot2, valid2, normed, normed_t, cot_t, inverse, proj, gatt, att, grads,
    terms, plane_in, acc, z_in, red, zfin, fin, mixed_out, gn_out, mixed_in, gn_in, gn_own,
    g_send, g_recv, s_send, s_recv, p_send, p_recv, z_send, z_recv, a_send, a_recv, f_send, f_recv,
):
    dp, blk = lax.axis_index("dp"), lax.axis_index("blk")
    xl, z = dp // NZ, dp % NZ
    y, xh, c = blk // 4, (blk // 2) % 2, blk % 2
    x = xh * 2 + xl
    sibling = device(x, y, z, 1 - c)

    def gather_to(cross, dy, dc):
        tx = 3 - x if cross else x
        return device(tx, (y + dy) % NY, z, (c + dc) % 2), (c + dc) % 2

    barrier = pltpu.get_barrier_semaphore()
    greet = [gather_to(*o)[0] for o in GATHER]
    greet += [device((x + dx) % NX, (y + dy) % NY, z, c) for dx, dy in PLANE]
    greet += [device(x, y, (z + dz) % NZ, c) for dz in range(1, NZ)]
    greet += [device(xh * 2 + 1 - xl, y, z, t) for t in range(2)]
    for d in greet:
        pl.semaphore_signal(barrier, inc=1, device_id=d, device_id_type=MESH)

    for h in range(2):
        for part in range(3):
            stage[h, :, part * HALF : (part + 1) * HALF] = win_ref[:, part * 2 * HALF + h * HALF : part * 2 * HALF + (h + 1) * HALF]
        stage[h, :, 3 * HALF :] = wout_ref[:, h * HALF : (h + 1) * HALF]
    my_rows = pl.ds(pl.multiple_of(blk * 64, 64), 64)

    def copy(src, dst, ss, rs, to):
        return pltpu.make_async_remote_copy(src_ref=src, dst_ref=dst, send_sem=ss, recv_sem=rs, device_id=to, device_id_type=MESH)

    def normalise(src, at):
        @pl.loop(0, 2)
        def _(i):
            rows = pl.ds(pl.multiple_of(i * 128, 128), 128)
            out = pl.ds(pl.multiple_of(at + i * 128, 128), 128)
            floats = src[rows, :].astype(F32)
            inv = lax.rsqrt(jnp.mean(floats * floats, axis=-1, keepdims=True) + EPSILON)
            inverse[out, :] = jnp.broadcast_to(inv, (128, 128))
            normed[out, :] = (floats * inv).astype(BF)

    pl.semaphore_wait(barrier, len(greet))

    gathers = []
    for j, o in enumerate(GATHER):
        to, h = gather_to(*o)
        cp = copy(stage.at[h], w.at[my_rows], g_send.at[j], g_recv.at[j], to)
        cp.start()
        gathers.append(cp)
    shares = [
        copy(tok_ref, tok2, s_send.at[0], s_recv.at[0], sibling),
        copy(cot_ref, cot2, s_send.at[1], s_recv.at[1], sibling),
        copy(valid_ref, valid2, s_send.at[2], s_recv.at[2], sibling),
    ]
    for cp in shares:
        cp.start()
    w[my_rows, :] = stage[c]

    normalise(tok_ref, 0)
    for cp in shares:
        cp.wait()
    normalise(tok2, ROWS)

    @pl.loop(0, 4)
    def _(i):
        cols = pl.ds(pl.multiple_of(i * 256, 256), 256)
        normed_t[cols, :] = normed[:, cols].T
        cot_t[cols, 0:ROWS] = cot_ref[:, cols].T
        cot_t[cols, ROWS:] = cot2[:, cols].T

    for cp in gathers:
        cp.wait()

    @pl.loop(0, 3)
    def _(i):
        cols = pl.ds(pl.multiple_of(i * 256, 256), 256)
        for r in range(2):
            proj[r * 256 : (r + 1) * 256, cols] = dot(normed[r * 256 : (r + 1) * 256, :], w[:, cols], 1, 0).astype(BF)

    for r, src in enumerate((cot_ref, cot2)):
        gatt[r * 256 : (r + 1) * 256, :] = dot(src[...], w[:, 3 * HALF :], 1, 0).astype(BF)

    row_at = lax.broadcasted_iota(jnp.int32, (TILE, TILE), 0)
    col_at = lax.broadcasted_iota(jnp.int32, (TILE, TILE), 1)
    causal = (row_at // CAPLEN == col_at // CAPLEN) & (col_at <= row_at)
    scale = HEAD_SIZE ** (-0.5)

    for side, real in enumerate((valid_ref, valid2)):
        @pl.loop(0, ROWS // TILE)
        def _(t):
            rows = pl.ds(pl.multiple_of(side * ROWS + t * TILE, TILE), TILE)
            keys_real = real[0:1, pl.ds(pl.multiple_of(t * TILE, TILE), TILE)]
            allowed = causal & (keys_real > 0.5)
            for h in range(4):
                q = proj[rows, h * 64 : (h + 1) * 64]
                k = proj[rows, HALF + h * 64 : HALF + (h + 1) * 64]
                v = proj[rows, 2 * HALF + h * 64 : 2 * HALF + (h + 1) * 64]
                g = gatt[rows, h * 64 : (h + 1) * 64]
                raised = jnp.where(allowed, jnp.exp(dot(q, k, 1, 1) * scale), 0.0)
                prob = raised / jnp.sum(raised, axis=-1, keepdims=True)
                rounded = prob.astype(BF)
                att[rows, h * 64 : (h + 1) * 64] = dot(rounded, v, 1, 0).astype(BF)
                grad_prob = dot(g, v, 1, 1)
                mean = jnp.sum(prob * grad_prob, axis=-1, keepdims=True)
                grad_scores = (prob * (grad_prob - mean) * scale).astype(BF)
                grads[rows, h * 64 : (h + 1) * 64] = dot(grad_scores, k, 1, 0).astype(BF)
                grads[rows, HALF + h * 64 : HALF + (h + 1) * 64] = dot(grad_scores, q, 0, 0).astype(BF)
                grads[rows, 2 * HALF + h * 64 : 2 * HALF + (h + 1) * 64] = dot(rounded, g, 0, 0).astype(BF)

    @pl.loop(0, 4)
    def _(i):
        rows = pl.ds(pl.multiple_of(i * 256, 256), 256)
        for j in range(3):
            terms[rows, j * 256 : (j + 1) * 256] = dot(normed_t[rows, :], grads[:, j * 256 : (j + 1) * 256], 1, 0).astype(BF)
        terms[rows, 3 * HALF :] = dot(cot_t[rows, :], att[...], 1, 0).astype(BF)

    def piece(tx, ty):
        return pl.ds(pl.multiple_of((ty * 4 + tx) * 64, 64), 64)

    plane = []
    for j, (dx, dy) in enumerate(PLANE):
        tx, ty = (x + dx) % NX, (y + dy) % NY
        cp = copy(terms.at[piece(tx, ty)], plane_in.at[j], p_send.at[j], p_recv.at[j], device(tx, ty, z, c))
        cp.start()
        plane.append(cp)

    @pl.loop(0, 4)
    def _(i):
        cols = pl.ds(pl.multiple_of(i * 256, 256), 256)
        mixed_out[:, cols] = dot(att[ROWS:, :], w[cols, 3 * HALF :], 1, 1).astype(BF)
        gn_out[:, cols] = dot(grads[ROWS:, :], w[cols, : 3 * HALF], 1, 1).astype(BF)

    backs = [
        copy(mixed_out, mixed_in, s_send.at[3], s_recv.at[3], sibling),
        copy(gn_out, gn_in, s_send.at[4], s_recv.at[4], sibling),
    ]
    for cp in backs:
        cp.start()

    @pl.loop(0, 4)
    def _(i):
        cols = pl.ds(pl.multiple_of(i * 256, 256), 256)
        mixed_out_own = dot(att[:ROWS, :], w[cols, 3 * HALF :], 1, 1)
        lo_ref[:, cols] = (tok_ref[:, cols].astype(F32) + mixed_out_own).astype(BF)
        gn_own[:, cols] = dot(grads[:ROWS, :], w[cols, : 3 * HALF], 1, 1)

    for cp in backs:
        cp.wait()

    @pl.loop(0, 4)
    def _(i):
        rows = pl.ds(pl.multiple_of(i * 64, 64), 64)
        floats = tok_ref[rows, :].astype(F32)
        inv = inverse[rows, 0:1]
        grad_normed = gn_own[rows, :] + gn_in[rows, :].astype(F32)
        mean = jnp.mean(grad_normed * floats, axis=-1, keepdims=True)
        gt_ref[rows, :] = (cot_ref[rows, :].astype(F32) + inv * grad_normed - floats * (inv * inv * inv * mean)).astype(BF)
        lo_ref[rows, :] = (lo_ref[rows, :].astype(F32) + mixed_in[rows, :].astype(F32)).astype(BF)

    for cp in plane:
        cp.wait()

    for rg in range(4):
        mine = pl.ds(pl.multiple_of((y * 4 + x) * 64 + rg * 16, 16), 16)
        for cg in range(4):
            cols = slice(cg * 256, (cg + 1) * 256)
            total = terms[mine, cols].astype(F32)
            for j in range(len(PLANE)):
                total = total + plane_in[j, rg * 16 : (rg + 1) * 16, cols].astype(F32)
            acc[rg * 4 + cg] = total.astype(BF)

    lines = []
    for dz in range(1, NZ):
        tz = (z + dz) % NZ
        cp = copy(acc.at[tz], z_in.at[dz - 1], z_send.at[dz - 1], z_recv.at[dz - 1], device(x, y, tz, c))
        cp.start()
        lines.append(cp)
    for cp in lines:
        cp.wait()
    total = acc[z].astype(F32)
    for j in range(NZ - 1):
        total = total + z_in[j].astype(F32)
    red[...] = total.astype(BF)
    zfin[z] = total.astype(BF)

    lines = []
    for dz in range(1, NZ):
        tz = (z + dz) % NZ
        cp = copy(red, zfin.at[z], a_send.at[dz - 1], a_recv.at[dz - 1], device(x, y, tz, c))
        cp.start()
        lines.append(cp)
    for cp in lines:
        cp.wait()

    across = copy(zfin, fin.at[c], f_send.at[0], f_recv.at[c], device(xh * 2 + 1 - xl, y, z, xl))
    beside = copy(zfin, fin.at[c], f_send.at[1], f_recv.at[c], sibling)
    across.start()

    @pl.when(c != xl)
    def _():
        beside.start()

    @pl.when(c == xl)
    def _():
        fin[c] = zfin[...]
        copy(zfin, fin.at[1 - c], f_send.at[1], f_recv.at[1 - c], sibling).wait_recv()

    @pl.when(c != xl)
    def _():
        for h in range(2):
            copy(zfin, fin.at[h], f_send.at[1], f_recv.at[h], sibling).wait_recv()
        beside.wait_send()

    across.wait_send()

    for h in range(2):
        for s in range(16):
            rg, cg = s // 4, s % 4
            rows = slice(rg * 16, (rg + 1) * 16)
            value = fin[h, s].astype(F32)
            if cg < 3:
                gin_ref[rows, cg * 512 + h * 256 : cg * 512 + (h + 1) * 256] = value
            else:
                gout_ref[rows, h * 256 : (h + 1) * 256] = value


def per_device(tokens, lengths, cotangent, input_weight, output_weight):
    real = jnp.arange(CAPLEN, dtype=jnp.int32)[None, :] < lengths[:, None]
    valid = jnp.broadcast_to(real.astype(F32).reshape(1, ROWS), (8, ROWS))
    vmem = pl.BlockSpec(memory_space=pltpu.VMEM)
    dma = pltpu.SemaphoreType.DMA
    n_g, n_p, n_z = len(GATHER), len(PLANE), NZ - 1
    return pl.pallas_call(
        kernel,
        out_shape=(
            jax.ShapeDtypeStruct((ROWS, D), BF),
            jax.ShapeDtypeStruct((ROWS, D), BF),
            jax.ShapeDtypeStruct((64, 1536), F32),
            jax.ShapeDtypeStruct((64, 512), F32),
        ),
        in_specs=[vmem] * 5,
        out_specs=(vmem,) * 4,
        scratch_shapes=[
            pltpu.VMEM((2, 64, D), BF),
            pltpu.VMEM((D, D), BF),
            pltpu.VMEM((ROWS, D), BF),
            pltpu.VMEM((ROWS, D), BF),
            pltpu.VMEM((8, ROWS), F32),
            pltpu.VMEM((2 * ROWS, D), BF),
            pltpu.VMEM((D, 2 * ROWS), BF),
            pltpu.VMEM((D, 2 * ROWS), BF),
            pltpu.VMEM((2 * ROWS, 128), F32),
            pltpu.VMEM((2 * ROWS, 3 * HALF), BF),
            pltpu.VMEM((2 * ROWS, HALF), BF),
            pltpu.VMEM((2 * ROWS, HALF), BF),
            pltpu.VMEM((2 * ROWS, 3 * HALF), BF),
            pltpu.VMEM((D, D), BF),
            pltpu.VMEM((n_p, 64, D), BF),
            pltpu.VMEM((16, 16, 256), BF),
            pltpu.VMEM((n_z, 16, 256), BF),
            pltpu.VMEM((16, 256), BF),
            pltpu.VMEM((16, 16, 256), BF),
            pltpu.VMEM((2, 16, 16, 256), BF),
            pltpu.VMEM((ROWS, D), BF),
            pltpu.VMEM((ROWS, D), BF),
            pltpu.VMEM((ROWS, D), BF),
            pltpu.VMEM((ROWS, D), BF),
            pltpu.VMEM((ROWS, D), F32),
            dma((n_g,)), dma((n_g,)),
            dma((5,)), dma((5,)),
            dma((n_p,)), dma((n_p,)),
            dma((n_z,)), dma((n_z,)),
            dma((n_z,)), dma((n_z,)),
            dma((2,)), dma((2,)),
        ],
        compiler_params=pltpu.CompilerParams(collective_id=0, has_side_effects=True, vmem_limit_bytes=50 * 2**20),
        name="layer",
    )(tokens, cotangent, valid, input_weight, output_weight)


def solution(mesh):
    placed = (
        P(("dp", "blk"), None),
        P(("dp", "blk")),
        P(("dp", "blk"), None),
        P("blk", None),
        P("blk", None),
    )
    return jax.shard_map(
        per_device,
        mesh=mesh,
        in_specs=placed,
        out_specs=(P(("dp", "blk"), None), P(("dp", "blk"), None), P("blk", None), P("blk", None)),
        check_vma=False,
    )
```

```python
import functools

import jax
import jax.numpy as jnp
from jax import lax
from jax.experimental import pallas as pl
from jax.experimental.pallas import tpu as pltpu
from jax.sharding import PartitionSpec as P

HEADS = 8
HEAD_SIZE = 64
CAPLEN = 32
EPSILON = 1e-06

MESH = pl.DeviceIdType.MESH
NX, NY, NZ = 4, 4, 16
ROWS = 256
D = 1024
HALF = 256
TILE = 128
BF = jnp.bfloat16
F32 = jnp.float32

GATHER = [(cross, dy, dc) for cross in (0, 1) for dy in range(4) for dc in range(2) if cross or dy or dc]


def device(x, y, z, c):
    return {"dp": (x % 2) * NZ + z, "blk": y * 4 + (x // 2) * 2 + c}


def dot(a, b, ca, cb):
    return lax.dot_general(a, b, (((ca,), (cb,)), ((), ())), preferred_element_type=F32)


def kernel(
    tok_hbm, cot_hbm, valid_ref, win_hbm, wout_hbm,
    lo_ref, gt_ref, gin_ref, gout_ref,
    tok_ref, cot_ref, win_ref, wout_ref,
    stage, w, tok2, cot2, valid2, normed, normed_t, cot_t, inverse, proj, gatt, att, grads,
    terms, first_in, first_sum, second_in, acc, z_in, red, fin, mixed_out, gn_out, mixed_in, gn_in, gn_own,
    l_sem, g_send, g_recv, s_send, s_recv, p_send, p_recv, q_send, q_recv, z_send, z_recv, f_send, f_recv,
):
    dp, blk = lax.axis_index("dp"), lax.axis_index("blk")
    xl, z = dp // NZ, dp % NZ
    y, xh, c = blk // 4, (blk // 2) % 2, blk % 2
    x = xh * 2 + xl
    sibling = device(x, y, z, 1 - c)

    loads = []
    for j, (src, dst) in enumerate(((win_hbm, win_ref), (wout_hbm, wout_ref), (tok_hbm, tok_ref), (cot_hbm, cot_ref))):
        cp = pltpu.make_async_copy(src, dst, l_sem.at[j])
        cp.start()
        loads.append(cp)

    def gather_to(cross, dy, dc):
        tx = 3 - x if cross else x
        return device(tx, (y + dy) % NY, z, (c + dc) % 2), (c + dc) % 2

    barrier = pltpu.get_barrier_semaphore()
    greet = [gather_to(*o)[0] for o in GATHER]
    greet += [device((x + d) % NX, y, z, c) for d in (1, 2, 3)]
    greet += [device(xh * 2 + t, y, (z + dz) % NZ, e) for dz in range(1, NZ) for t in range(2) for e in range(2)]
    greet += [device(xh * 2 + 1 - xl, y, z, t) for t in range(2)]
    for d in greet:
        pl.semaphore_signal(barrier, inc=1, device_id=d, device_id_type=MESH)

    def copy(src, dst, ss, rs, to):
        return pltpu.make_async_remote_copy(src_ref=src, dst_ref=dst, send_sem=ss, recv_sem=rs, device_id=to, device_id_type=MESH)

    loads[0].wait()
    loads[1].wait()
    for h in range(2):
        for i in range(2):
            for part in range(3):
                at = part * 2 * HALF + h * HALF + i * 128
                stage[h, i, :, part * 128 : (part + 1) * 128] = win_ref[:, at : at + 128]
            at = h * HALF + i * 128
            stage[h, i, :, 384:] = wout_ref[:, at : at + 128]
    my_rows = pl.ds(pl.multiple_of(blk * 64, 64), 64)
    for i in range(2):
        w[i, my_rows, :] = stage[c, i]

    def normalise(src, other, at):
        @pl.loop(0, 2)
        def _(i):
            rows = pl.ds(pl.multiple_of(i * 128, 128), 128)
            out = pl.ds(pl.multiple_of(at + i * 128, 128), 128)
            floats = src[rows, :].astype(F32)
            inv = lax.rsqrt(jnp.mean(floats * floats, axis=-1, keepdims=True) + EPSILON)
            inverse[out, :] = jnp.broadcast_to(inv, (128, 128))
            normed[out, :] = (floats * inv).astype(BF)

        @pl.loop(0, 4)
        def _(i):
            cols = pl.ds(pl.multiple_of(i * 256, 256), 256)
            normed_t[cols, at : at + ROWS] = normed[at : at + ROWS, cols].T
            cot_t[cols, at : at + ROWS] = other[:, cols].T

    loads[2].wait()
    loads[3].wait()
    normalise(tok_ref, cot_ref, 0)

    pl.semaphore_wait(barrier, len(greet))

    shares = [
        copy(tok_ref, tok2, s_send.at[0], s_recv.at[0], sibling),
        copy(cot_ref, cot2, s_send.at[1], s_recv.at[1], sibling),
        copy(valid_ref, valid2, s_send.at[2], s_recv.at[2], sibling),
    ]
    for cp in shares:
        cp.start()
    gathers = []
    for i in range(2):
        for j, o in enumerate(GATHER):
            to, h = gather_to(*o)
            cp = copy(stage.at[h, i], w.at[i, my_rows], g_send.at[i, j], g_recv.at[i, j], to)
            cp.start()
            gathers.append(cp)

    for cp in shares:
        cp.wait()
    normalise(tok2, cot2, ROWS)

    row_at = lax.broadcasted_iota(jnp.int32, (TILE, TILE), 0)
    col_at = lax.broadcasted_iota(jnp.int32, (TILE, TILE), 1)
    causal = (row_at // CAPLEN == col_at // CAPLEN) & (col_at <= row_at)
    scale = HEAD_SIZE ** (-0.5)

    def attend(i):
        for r, src in enumerate((cot_ref, cot2)):
            own = slice(r * 256, (r + 1) * 256)
            proj[own, :] = dot(normed[own, :], w[i, :, :384], 1, 0).astype(BF)
            gatt[own, :] = dot(src[...], w[i, :, 384:], 1, 0).astype(BF)
        for side, real in enumerate((valid_ref, valid2)):
            @pl.loop(0, ROWS // TILE)
            def _(t):
                rows = pl.ds(pl.multiple_of(side * ROWS + t * TILE, TILE), TILE)
                keys_real = real[0:1, pl.ds(pl.multiple_of(t * TILE, TILE), TILE)]
                allowed = causal & (keys_real > 0.5)
                for h in range(2):
                    q = proj[rows, h * 64 : (h + 1) * 64]
                    k = proj[rows, 128 + h * 64 : 128 + (h + 1) * 64]
                    v = proj[rows, 256 + h * 64 : 256 + (h + 1) * 64]
                    g = gatt[rows, h * 64 : (h + 1) * 64]
                    raised = jnp.where(allowed, jnp.exp(dot(q, k, 1, 1) * scale), 0.0)
                    prob = raised / jnp.sum(raised, axis=-1, keepdims=True)
                    rounded = prob.astype(BF)
                    att[i, rows, h * 64 : (h + 1) * 64] = dot(rounded, v, 1, 0).astype(BF)
                    grad_prob = dot(g, v, 1, 1)
                    mean = jnp.sum(prob * grad_prob, axis=-1, keepdims=True)
                    grad_scores = (prob * (grad_prob - mean) * scale).astype(BF)
                    grads[i, rows, h * 64 : (h + 1) * 64] = dot(grad_scores, k, 1, 0).astype(BF)
                    grads[i, rows, 128 + h * 64 : 128 + (h + 1) * 64] = dot(grad_scores, q, 0, 0).astype(BF)
                    grads[i, rows, 256 + h * 64 : 256 + (h + 1) * 64] = dot(rounded, g, 0, 0).astype(BF)

    def products(i):
        @pl.loop(0, 4)
        def _(t):
            rows = pl.ds(pl.multiple_of(t * 256, 256), 256)
            terms[i, 0, t] = dot(normed_t[rows, :], grads[i, :, :256], 1, 0).astype(BF).reshape(4, 64, 256)
            terms[i, 1, t, :, :, :128] = dot(normed_t[rows, :], grads[i, :, 256:], 1, 0).astype(BF).reshape(4, 64, 128)
            terms[i, 1, t, :, :, 128:] = dot(cot_t[rows, :], att[i], 1, 0).astype(BF).reshape(4, 64, 128)

    def first_start(i):
        started = []
        for d in (1, 2, 3):
            tx, ty = (x + d) % NX, (y + d) % NY
            started.append(copy(terms.at[i, 0, :, tx], first_in.at[i, 0, d - 1], p_send.at[i, 0, d - 1], p_recv.at[i, 0, d - 1], device(tx, y, z, c)))
            started.append(copy(terms.at[i, 1, ty], first_in.at[i, 1, d - 1], p_send.at[i, 1, d - 1], p_recv.at[i, 1, d - 1], device(x, ty, z, c)))
        for cp in started:
            cp.start()
        return started

    def first_end(i, started):
        for cp in started:
            cp.wait()
        for g in range(4):
            for part in range(2):
                total = (terms[i, 0, g, x] if part == 0 else terms[i, 1, y, g]).astype(F32)
                for d in range(3):
                    total = total + first_in[i, part, d, g].astype(F32)
                first_sum[i, part, g] = total.astype(BF)
        started = []
        for d in (1, 2, 3):
            tx, ty = (x + d) % NX, (y + d) % NY
            started.append(copy(first_sum.at[i, 0, ty], second_in.at[i, 0, d - 1], q_send.at[i, 0, d - 1], q_recv.at[i, 0, d - 1], device(x, ty, z, c)))
            started.append(copy(first_sum.at[i, 1, tx], second_in.at[i, 1, d - 1], q_send.at[i, 1, d - 1], q_recv.at[i, 1, d - 1], device(tx, y, z, c)))
        for cp in started:
            cp.start()
        return started

    def second_end(i, started):
        for cp in started:
            cp.wait()
        for part in range(2):
            total = first_sum[i, part, y if part == 0 else x].astype(F32)
            for d in range(3):
                total = total + second_in[i, part, d].astype(F32)
            total = total.astype(BF)
            for g in range(4):
                for h in range(2):
                    acc[i, g * 4 + part * 2 + h] = total[g * 16 : (g + 1) * 16, h * 128 : (h + 1) * 128]
        started = []
        for dz in range(1, NZ):
            tz = (z + dz) % NZ
            started.append(copy(acc.at[i, tz], z_in.at[i, dz - 1], z_send.at[i, dz - 1], z_recv.at[i, dz - 1], device(x, y, tz, c)))
        for cp in started:
            cp.start()
        return started

    def line_end(i, started):
        for cp in started:
            cp.wait()
        total = acc[i, z].astype(F32)
        for j in range(NZ - 1):
            total = total + z_in[i, j].astype(F32)
        red[i] = total.astype(BF)
        started = []
        for dz in range(NZ):
            tz = (z + dz) % NZ
            for other in range(2):
                if dz or other:
                    tx = xh * 2 + (xl + other) % 2
                    started.append(copy(red.at[i], fin.at[i, c, z], f_send.at[i, dz, other], f_recv.at[i], device(tx, y, tz, xl)))
        for cp in started:
            cp.start()
        beside = copy(red.at[i], fin.at[i, c, z], f_send.at[i, 0, 0], f_recv.at[i], sibling)
        here = pltpu.make_async_copy(red.at[i], fin.at[i, c, z], f_recv.at[i])

        @pl.when(c != xl)
        def _():
            beside.start()

        @pl.when(c == xl)
        def _():
            here.start()

        return started, beside

    def back_end(i, started, beside):
        pltpu.make_async_copy(fin.at[i], fin.at[i], f_recv.at[i]).wait()
        for h in range(2):
            for s in range(16):
                rows = slice(s // 4 * 16, (s // 4 + 1) * 16)
                part = s % 4
                at = h * HALF + i * 128
                value = fin[i, h, s].astype(F32)
                if part < 3:
                    gin_ref[rows, part * 512 + at : part * 512 + at + 128] = value
                else:
                    gout_ref[rows, at : at + 128] = value
        for cp in started:
            cp.wait_send()

        @pl.when(c != xl)
        def _():
            beside.wait_send()

    for cp in gathers[: len(GATHER)]:
        cp.wait()
    attend(0)
    products(0)
    first0 = first_start(0)
    for cp in gathers[len(GATHER) :]:
        cp.wait()
    attend(1)
    products(1)
    first1 = first_start(1)
    second0 = first_end(0, first0)

    def head_sums(rows, cols):
        mixed = dot(att[0, rows, :], w[0, cols, 384:], 1, 1) + dot(att[1, rows, :], w[1, cols, 384:], 1, 1)
        back = dot(grads[0, rows, :], w[0, cols, :384], 1, 1) + dot(grads[1, rows, :], w[1, cols, :384], 1, 1)
        return mixed, back

    @pl.loop(0, 4)
    def _(t):
        cols = pl.ds(pl.multiple_of(t * 256, 256), 256)
        mixed, back = head_sums(slice(ROWS, 2 * ROWS), cols)
        mixed_out[:, cols] = mixed.astype(BF)
        gn_out[:, cols] = back.astype(BF)

    backs = [
        copy(mixed_out, mixed_in, s_send.at[3], s_recv.at[3], sibling),
        copy(gn_out, gn_in, s_send.at[4], s_recv.at[4], sibling),
    ]
    for cp in backs:
        cp.start()
    line0 = second_end(0, second0)
    second1 = first_end(1, first1)

    @pl.loop(0, 4)
    def _(t):
        cols = pl.ds(pl.multiple_of(t * 256, 256), 256)
        mixed, back = head_sums(slice(0, ROWS), cols)
        lo_ref[:, cols] = (tok_ref[:, cols].astype(F32) + mixed).astype(BF)
        gn_own[:, cols] = back

    line1 = second_end(1, second1)
    back0 = line_end(0, line0)

    for cp in backs:
        cp.wait()

    @pl.loop(0, 4)
    def _(t):
        rows = pl.ds(pl.multiple_of(t * 64, 64), 64)
        floats = tok_ref[rows, :].astype(F32)
        inv = inverse[rows, 0:1]
        grad_normed = gn_own[rows, :] + gn_in[rows, :].astype(F32)
        mean = jnp.mean(grad_normed * floats, axis=-1, keepdims=True)
        gt_ref[rows, :] = (cot_ref[rows, :].astype(F32) + inv * grad_normed - floats * (inv * inv * inv * mean)).astype(BF)
        lo_ref[rows, :] = (lo_ref[rows, :].astype(F32) + mixed_in[rows, :].astype(F32)).astype(BF)

    back1 = line_end(1, line1)
    back_end(0, *back0)
    back_end(1, *back1)


def per_device(tokens, lengths, cotangent, input_weight, output_weight):
    real = jnp.arange(CAPLEN, dtype=jnp.int32)[None, :] < lengths[:, None]
    valid = jnp.broadcast_to(real.astype(F32).reshape(1, ROWS), (8, ROWS))
    vmem, anywhere = pl.BlockSpec(memory_space=pltpu.VMEM), pl.BlockSpec(memory_space=pl.ANY)
    dma = pltpu.SemaphoreType.DMA
    n_g, n_z = len(GATHER), NZ - 1
    return pl.pallas_call(
        kernel,
        out_shape=(
            jax.ShapeDtypeStruct((ROWS, D), BF),
            jax.ShapeDtypeStruct((ROWS, D), BF),
            jax.ShapeDtypeStruct((64, 1536), F32),
            jax.ShapeDtypeStruct((64, 512), F32),
        ),
        in_specs=[anywhere, anywhere, vmem, anywhere, anywhere],
        out_specs=(vmem,) * 4,
        scratch_shapes=[
            pltpu.VMEM((ROWS, D), BF),
            pltpu.VMEM((ROWS, D), BF),
            pltpu.VMEM((64, 1536), BF),
            pltpu.VMEM((64, 512), BF),
            pltpu.VMEM((2, 2, 64, 512), BF),
            pltpu.VMEM((2, D, 512), BF),
            pltpu.VMEM((ROWS, D), BF),
            pltpu.VMEM((ROWS, D), BF),
            pltpu.VMEM((8, ROWS), F32),
            pltpu.VMEM((2 * ROWS, D), BF),
            pltpu.VMEM((D, 2 * ROWS), BF),
            pltpu.VMEM((D, 2 * ROWS), BF),
            pltpu.VMEM((2 * ROWS, 128), F32),
            pltpu.VMEM((2 * ROWS, 384), BF),
            pltpu.VMEM((2 * ROWS, 128), BF),
            pltpu.VMEM((2, 2 * ROWS, 128), BF),
            pltpu.VMEM((2, 2 * ROWS, 384), BF),
            pltpu.VMEM((2, 2, 4, 4, 64, 256), BF),
            pltpu.VMEM((2, 2, 3, 4, 64, 256), BF),
            pltpu.VMEM((2, 2, 4, 64, 256), BF),
            pltpu.VMEM((2, 2, 3, 64, 256), BF),
            pltpu.VMEM((2, 16, 16, 128), BF),
            pltpu.VMEM((2, n_z, 16, 128), BF),
            pltpu.VMEM((2, 16, 128), BF),
            pltpu.VMEM((2, 2, 16, 16, 128), BF),
            pltpu.VMEM((ROWS, D), BF),
            pltpu.VMEM((ROWS, D), BF),
            pltpu.VMEM((ROWS, D), BF),
            pltpu.VMEM((ROWS, D), BF),
            pltpu.VMEM((ROWS, D), F32),
            dma((4,)),
            dma((2, n_g)), dma((2, n_g)),
            dma((5,)), dma((5,)),
            dma((2, 2, 3)), dma((2, 2, 3)),
            dma((2, 2, 3)), dma((2, 2, 3)),
            dma((2, n_z)), dma((2, n_z)),
            dma((2, NZ, 2)), dma((2,)),
        ],
        compiler_params=pltpu.CompilerParams(collective_id=0, has_side_effects=True, vmem_limit_bytes=50 * 2**20),
        name="layer",
    )(tokens, cotangent, valid, input_weight, output_weight)


def solution(mesh):
    placed = (
        P(("dp", "blk"), None),
        P(("dp", "blk")),
        P(("dp", "blk"), None),
        P("blk", None),
        P("blk", None),
    )
    return jax.shard_map(
        per_device,
        mesh=mesh,
        in_specs=placed,
        out_specs=(P(("dp", "blk"), None), P(("dp", "blk"), None), P("blk", None), P("blk", None)),
        check_vma=False,
    )
```

```python
import functools

import jax
import jax.numpy as jnp
from jax import lax
from jax.experimental import pallas as pl
from jax.experimental.pallas import tpu as pltpu
from jax.sharding import PartitionSpec as P

HEADS = 8
HEAD_SIZE = 64
CAPLEN = 32
EPSILON = 1e-06

MESH = pl.DeviceIdType.MESH
NX, NY, NZ = 4, 4, 16
ROWS = 256
D = 1024
HALF = 256
TILE = 128
BF = jnp.bfloat16
F32 = jnp.float32

GATHER = [(0, 1, 0), (0, 3, 0), (1, 0, 0), (0, 1, 1), (0, 3, 1), (1, 0, 1), (1, 1, 0), (1, 3, 0), (1, 1, 1), (1, 3, 1)]
GATHER += [(0, 2, 0), (0, 2, 1), (1, 2, 0), (1, 2, 1)]
N_G = len(GATHER)


def device(x, y, z, c):
    return {"dp": (x % 2) * NZ + z, "blk": y * 4 + (x // 2) * 2 + c}


def dot(a, b, ca, cb):
    return lax.dot_general(a, b, (((ca,), (cb,)), ((), ())), preferred_element_type=F32)


def kernel(
    tok_hbm, cot_hbm, valid_ref, win_hbm, wout_hbm,
    lo_ref, gt_ref, gin_ref, gout_ref,
    tok_ref, cot_ref, win_ref, wout_ref,
    stage, w, tok2, cot2, valid2, normed, normed_t, cot_t, inverse, proj, gatt, att, grads,
    terms, first_in, first_sum, second_in, acc, z_in, red, fin, mixed_out, gn_out, mixed_in, gn_in, gn_own,
    l_sem, ready, g_send, g_recv, h_send, h_recv, w_send, w_recv, s_send, s_recv, p_send, p_recv, q_send, q_recv, z_send, z_recv, f_send, f_recv,
):
    dp, blk = lax.axis_index("dp"), lax.axis_index("blk")
    xl, z = dp // NZ, dp % NZ
    y, xh, c = blk // 4, (blk // 2) % 2, blk % 2
    x = xh * 2 + xl
    sibling = device(x, y, z, 1 - c)

    loads = []
    for j, (src, dst) in enumerate(((win_hbm, win_ref), (wout_hbm, wout_ref), (tok_hbm, tok_ref), (cot_hbm, cot_ref))):
        cp = pltpu.make_async_copy(src, dst, l_sem.at[j])
        cp.start()
        loads.append(cp)

    def gather_to(cross, dy, dc):
        tx = 3 - x if cross else x
        return device(tx, (y + dy) % NY, z, (c + dc) % 2), (c + dc) % 2

    barrier = pltpu.get_barrier_semaphore()
    greet = [gather_to(*o)[0] for o in GATHER] + [sibling]
    greet += [device((x + d) % NX, y, z, c) for d in (1, 2, 3)]
    greet += [device(x, y, (z + d) % NZ, c) for d in (1, NZ - 1)]
    greet += [device(xh * 2 + 1 - xl, y, z, 1 - c)]
    for d in greet:
        pl.semaphore_signal(barrier, inc=1, device_id=d, device_id_type=MESH)

    def ready_signal(k):
        for d in (1 << k, NZ - (1 << k)):
            pl.semaphore_signal(ready.at[k], inc=1, device_id=device(x, y, (z + d) % NZ, c), device_id_type=MESH)

    def ready_wait(k):
        pl.semaphore_wait(ready.at[k], 2)

    def copy(src, dst, ss, rs, to):
        return pltpu.make_async_remote_copy(src_ref=src, dst_ref=dst, send_sem=ss, recv_sem=rs, device_id=to, device_id_type=MESH)

    loads[0].wait()
    loads[1].wait()
    for h in range(2):
        for i in range(2):
            for part in range(3):
                at = part * 2 * HALF + h * HALF + i * 128
                stage[h, i, :, part * 128 : (part + 1) * 128] = win_ref[:, at : at + 128]
            at = h * HALF + i * 128
            stage[h, i, :, 384:] = wout_ref[:, at : at + 128]
    my_rows = pl.ds(pl.multiple_of(blk * 64, 64), 64)
    for i in range(2):
        w[i, my_rows, :] = stage[c, i]

    def normalise(src, other, at):
        @pl.loop(0, 2)
        def _(i):
            rows = pl.ds(pl.multiple_of(i * 128, 128), 128)
            out = pl.ds(pl.multiple_of(at + i * 128, 128), 128)
            floats = src[rows, :].astype(F32)
            inv = lax.rsqrt(jnp.mean(floats * floats, axis=-1, keepdims=True) + EPSILON)
            inverse[out, :] = jnp.broadcast_to(inv, (128, 128))
            normed[out, :] = (floats * inv).astype(BF)

        @pl.loop(0, 4)
        def _(i):
            cols = pl.ds(pl.multiple_of(i * 256, 256), 256)
            normed_t[cols, at : at + ROWS] = normed[at : at + ROWS, cols].T
            cot_t[cols, at : at + ROWS] = other[:, cols].T

    loads[2].wait()
    loads[3].wait()
    normalise(tok_ref, cot_ref, 0)

    pl.semaphore_wait(barrier, len(greet))
    ready_signal(0)

    shares = [
        copy(tok_ref, tok2, s_send.at[0], s_recv.at[0], sibling),
        copy(cot_ref, cot2, s_send.at[1], s_recv.at[1], sibling),
        copy(valid_ref, valid2, s_send.at[2], s_recv.at[2], sibling),
    ]
    colour = (z + xl + xh) % 2
    half = pl.ds(pl.multiple_of(colour * 32, 32), 32)
    my_half = pl.ds(pl.multiple_of(blk * 64 + colour * 32, 32), 32)
    hand_to = [device(x, y, (z + 1) % NZ, c), device(x, y, (z + NZ - 1) % NZ, c), device(xh * 2 + 1 - xl, y, z, c)]

    def direct_start(i):
        started = []
        for j, o in enumerate(GATHER):
            to, h = gather_to(*o)
            started.append(copy(stage.at[h, i, half], w.at[i, my_half], g_send.at[i, j], g_recv.at[i, j], to))
        for cp in started:
            cp.start()
        return started

    def hand_start(i, j):
        cross, dy, dc = GATHER[j]
        block = (y + NY - dy) % NY * 4 + (1 - xh if cross else xh) * 2 + (c + dc) % 2
        rows = pl.ds(pl.multiple_of(block * 64 + colour * 32, 32), 32)
        cp = copy(w.at[i, rows], w.at[i, rows], h_send.at[i, j], h_recv.at[i, j], hand_to[j % 3])
        cp.start()
        return cp

    wides = [copy(stage.at[1 - c, i], w.at[i, my_rows], w_send.at[i], w_recv.at[i], sibling) for i in range(2)]
    direct0 = direct_start(0)
    shares[0].start()
    shares[1].start()
    shares[2].start()
    wides[0].start()
    wides[1].start()
    for cp in shares:
        cp.wait()
    ready_wait(0)
    ready_signal(1)
    hands0 = []
    for j in range(6):
        direct0[j].wait_recv()
        hands0.append(hand_start(0, j))
    direct1 = direct_start(1)
    for j in range(6, N_G):
        direct0[j].wait_recv()
        hands0.append(hand_start(0, j))
    normalise(tok2, cot2, ROWS)
    ready_wait(1)
    ready_signal(2)

    def gather_end(i, hands):
        for cp in hands:
            cp.wait_recv()
        wides[i].wait_recv()

    row_at = lax.broadcasted_iota(jnp.int32, (TILE, TILE), 0)
    col_at = lax.broadcasted_iota(jnp.int32, (TILE, TILE), 1)
    causal = (row_at // CAPLEN == col_at // CAPLEN) & (col_at <= row_at)
    scale = HEAD_SIZE ** (-0.5)

    first_head = lax.broadcasted_iota(jnp.int32, (TILE, 128), 1) < HEAD_SIZE

    def stack(pair):
        zero = jnp.zeros_like(pair)
        return jnp.concatenate([jnp.where(first_head, pair, zero), jnp.where(first_head, zero, pair)], axis=0)

    def unstack(both):
        return jnp.where(first_head, both[:TILE], both[TILE:])

    def project(i):
        for r, src in enumerate((cot_ref, cot2)):
            own = slice(r * 256, (r + 1) * 256)
            proj[own, :] = dot(normed[own, :], w[i, :, :384], 1, 0).astype(BF)
            gatt[own, :] = dot(src[...], w[i, :, 384:], 1, 0).astype(BF)

    def attend(i):
        tiles = [(side, t) for side in range(2) for t in range(ROWS // TILE)]
        rows = [slice(side * ROWS + t * TILE, side * ROWS + (t + 1) * TILE) for side, t in tiles]
        q = [stack(proj[r, :128]) for r in rows]
        k = [proj[r, 128:256] for r in rows]
        v = [proj[r, 256:] for r in rows]
        g = [stack(gatt[r, :]) for r in rows]
        scores = [dot(a, b, 1, 1) for a, b in zip(q, k)]
        grad_prob = [dot(a, b, 1, 1) for a, b in zip(g, v)]
        raised = []
        for (side, t), sc in zip(tiles, scores):
            keys_real = (valid_ref, valid2)[side][0:1, t * TILE : (t + 1) * TILE]
            allowed = causal & (keys_real > 0.5)
            raised.append(jnp.where(jnp.concatenate([allowed, allowed], axis=0), jnp.exp(sc * scale), 0.0))
        prob = [e / jnp.sum(e, axis=-1, keepdims=True) for e in raised]
        rounded = [p.astype(BF) for p in prob]
        for r, p, b in zip(rows, rounded, v):
            att[i, r, :] = unstack(dot(p, b, 1, 0)).astype(BF)
        for r, p, b in zip(rows, rounded, g):
            grads[i, r, 256:] = dot(p, b, 0, 0).astype(BF)
        grad_scores = [(p * (gp - jnp.sum(p * gp, axis=-1, keepdims=True)) * scale).astype(BF) for p, gp in zip(prob, grad_prob)]
        for r, gs, b in zip(rows, grad_scores, k):
            grads[i, r, :128] = unstack(dot(gs, b, 1, 0)).astype(BF)
        for r, gs, b in zip(rows, grad_scores, q):
            grads[i, r, 128:256] = dot(gs, b, 0, 0).astype(BF)

    def products(i):
        @pl.loop(0, 4)
        def _(t):
            rows = pl.ds(pl.multiple_of(t * 256, 256), 256)
            terms[i, 0, t] = dot(normed_t[rows, :], grads[i, :, :256], 1, 0).astype(BF).reshape(4, 64, 256)
            terms[i, 1, t, :, :, :128] = dot(normed_t[rows, :], grads[i, :, 256:], 1, 0).astype(BF).reshape(4, 64, 128)
            terms[i, 1, t, :, :, 128:] = dot(cot_t[rows, :], att[i], 1, 0).astype(BF).reshape(4, 64, 128)

    def first_start(i):
        started = []
        for d in (1, 2, 3):
            tx, ty = (x + d) % NX, (y + d) % NY
            started.append(copy(terms.at[i, 0, :, tx], first_in.at[i, 0, d - 1], p_send.at[i, 0, d - 1], p_recv.at[i, 0, d - 1], device(tx, y, z, c)))
            started.append(copy(terms.at[i, 1, ty], first_in.at[i, 1, d - 1], p_send.at[i, 1, d - 1], p_recv.at[i, 1, d - 1], device(x, ty, z, c)))
        for cp in started:
            cp.start()
        return started

    def first_end(i, started):
        for cp in started:
            cp.wait()
        for g in range(4):
            for part in range(2):
                total = (terms[i, 0, g, x] if part == 0 else terms[i, 1, y, g]).astype(F32)
                for d in range(3):
                    total = total + first_in[i, part, d, g].astype(F32)
                first_sum[i, part, g] = total.astype(BF)
        started = []
        for d in (1, 2, 3):
            tx, ty = (x + d) % NX, (y + d) % NY
            started.append(copy(first_sum.at[i, 0, ty], second_in.at[i, 0, d - 1], q_send.at[i, 0, d - 1], q_recv.at[i, 0, d - 1], device(x, ty, z, c)))
            started.append(copy(first_sum.at[i, 1, tx], second_in.at[i, 1, d - 1], q_send.at[i, 1, d - 1], q_recv.at[i, 1, d - 1], device(tx, y, z, c)))
        for cp in started:
            cp.start()
        return started

    def second_end(i, started):
        for cp in started:
            cp.wait()
        for part in range(2):
            total = first_sum[i, part, y if part == 0 else x].astype(F32)
            for d in range(3):
                total = total + second_in[i, part, d].astype(F32)
            total = total.astype(BF)
            for g in range(4):
                for h in range(2):
                    acc[i, g * 4 + part * 2 + h] = total[g * 16 : (g + 1) * 16, h * 128 : (h + 1) * 128]
        started = []
        for dz in range(1, NZ):
            tz = (z + dz) % NZ
            started.append(copy(acc.at[i, tz], z_in.at[i, dz - 1], z_send.at[i, dz - 1], z_recv.at[i, dz - 1], device(x, y, tz, c)))
        for cp in started:
            cp.start()
        return started

    def line_end(i, started):
        for cp in started:
            cp.wait()
        total = acc[i, z].astype(F32)
        for j in range(NZ - 1):
            total = total + z_in[i, j].astype(F32)
        red[i] = total.astype(BF)
        started = []
        for dz in range(NZ):
            tz = (z + dz) % NZ
            for other in range(2):
                if dz or other:
                    tx = xh * 2 + (xl + other) % 2
                    started.append(copy(red.at[i], fin.at[i, c, z], f_send.at[i, dz, other], f_recv.at[i], device(tx, y, tz, xl)))
        for cp in started:
            cp.start()
        beside = copy(red.at[i], fin.at[i, c, z], f_send.at[i, 0, 0], f_recv.at[i], sibling)
        here = pltpu.make_async_copy(red.at[i], fin.at[i, c, z], f_recv.at[i])

        @pl.when(c != xl)
        def _():
            beside.start()

        @pl.when(c == xl)
        def _():
            here.start()

        return started, beside

    def back_end(i, started, beside):
        pltpu.make_async_copy(fin.at[i], fin.at[i], f_recv.at[i]).wait()
        for h in range(2):
            for s in range(16):
                rows = slice(s // 4 * 16, (s // 4 + 1) * 16)
                part = s % 4
                at = h * HALF + i * 128
                value = fin[i, h, s].astype(F32)
                if part < 3:
                    gin_ref[rows, part * 512 + at : part * 512 + at + 128] = value
                else:
                    gout_ref[rows, at : at + 128] = value
        for cp in started:
            cp.wait_send()

        @pl.when(c != xl)
        def _():
            beside.wait_send()

    gather_end(0, hands0)
    project(0)
    hands1 = []
    for j in range(N_G):
        direct1[j].wait_recv()
        hands1.append(hand_start(1, j))
    attend(0)
    products(0)
    first0 = first_start(0)
    gather_end(1, hands1)
    project(1)
    attend(1)
    products(1)
    first1 = first_start(1)
    second0 = first_end(0, first0)
    ready_wait(2)

    def head_sums(rows, cols):
        mixed = dot(att[0, rows, :], w[0, cols, 384:], 1, 1) + dot(att[1, rows, :], w[1, cols, 384:], 1, 1)
        back = dot(grads[0, rows, :], w[0, cols, :384], 1, 1) + dot(grads[1, rows, :], w[1, cols, :384], 1, 1)
        return mixed, back

    @pl.loop(0, 4)
    def _(t):
        cols = pl.ds(pl.multiple_of(t * 256, 256), 256)
        mixed, back = head_sums(slice(ROWS, 2 * ROWS), cols)
        mixed_out[:, cols] = mixed.astype(BF)
        gn_out[:, cols] = back.astype(BF)

    backs = [
        copy(mixed_out, mixed_in, s_send.at[3], s_recv.at[3], sibling),
        copy(gn_out, gn_in, s_send.at[4], s_recv.at[4], sibling),
    ]
    for cp in backs:
        cp.start()
    line0 = second_end(0, second0)
    second1 = first_end(1, first1)

    @pl.loop(0, 4)
    def _(t):
        cols = pl.ds(pl.multiple_of(t * 256, 256), 256)
        mixed, back = head_sums(slice(0, ROWS), cols)
        lo_ref[:, cols] = (tok_ref[:, cols].astype(F32) + mixed).astype(BF)
        gn_own[:, cols] = back

    line1 = second_end(1, second1)
    back0 = line_end(0, line0)

    for cp in backs:
        cp.wait()

    @pl.loop(0, 4)
    def _(t):
        rows = pl.ds(pl.multiple_of(t * 64, 64), 64)
        floats = tok_ref[rows, :].astype(F32)
        inv = inverse[rows, 0:1]
        grad_normed = gn_own[rows, :] + gn_in[rows, :].astype(F32)
        mean = jnp.mean(grad_normed * floats, axis=-1, keepdims=True)
        gt_ref[rows, :] = (cot_ref[rows, :].astype(F32) + inv * grad_normed - floats * (inv * inv * inv * mean)).astype(BF)
        lo_ref[rows, :] = (lo_ref[rows, :].astype(F32) + mixed_in[rows, :].astype(F32)).astype(BF)

    back1 = line_end(1, line1)
    back_end(0, *back0)
    back_end(1, *back1)
    for cp in direct0 + direct1 + hands0 + hands1 + wides:
        cp.wait_send()


def per_device(tokens, lengths, cotangent, input_weight, output_weight):
    real = jnp.arange(CAPLEN, dtype=jnp.int32)[None, :] < lengths[:, None]
    valid = jnp.broadcast_to(real.astype(F32).reshape(1, ROWS), (8, ROWS))
    vmem, hbm = pl.BlockSpec(memory_space=pltpu.VMEM), pl.BlockSpec(memory_space=pltpu.HBM)
    dma = pltpu.SemaphoreType.DMA
    n_z = NZ - 1
    return pl.pallas_call(
        kernel,
        out_shape=(
            jax.ShapeDtypeStruct((ROWS, D), BF),
            jax.ShapeDtypeStruct((ROWS, D), BF),
            jax.ShapeDtypeStruct((64, 1536), F32),
            jax.ShapeDtypeStruct((64, 512), F32),
        ),
        in_specs=[hbm, hbm, vmem, hbm, hbm],
        out_specs=(vmem,) * 4,
        scratch_shapes=[
            pltpu.VMEM((ROWS, D), BF),
            pltpu.VMEM((ROWS, D), BF),
            pltpu.VMEM((64, 1536), BF),
            pltpu.VMEM((64, 512), BF),
            pltpu.VMEM((2, 2, 64, 512), BF),
            pltpu.VMEM((2, D, 512), BF),
            pltpu.VMEM((ROWS, D), BF),
            pltpu.VMEM((ROWS, D), BF),
            pltpu.VMEM((8, ROWS), F32),
            pltpu.VMEM((2 * ROWS, D), BF),
            pltpu.VMEM((D, 2 * ROWS), BF),
            pltpu.VMEM((D, 2 * ROWS), BF),
            pltpu.VMEM((2 * ROWS, 128), F32),
            pltpu.VMEM((2 * ROWS, 384), BF),
            pltpu.VMEM((2 * ROWS, 128), BF),
            pltpu.VMEM((2, 2 * ROWS, 128), BF),
            pltpu.VMEM((2, 2 * ROWS, 384), BF),
            pltpu.VMEM((2, 2, 4, 4, 64, 256), BF),
            pltpu.VMEM((2, 2, 3, 4, 64, 256), BF),
            pltpu.VMEM((2, 2, 4, 64, 256), BF),
            pltpu.VMEM((2, 2, 3, 64, 256), BF),
            pltpu.VMEM((2, 16, 16, 128), BF),
            pltpu.VMEM((2, n_z, 16, 128), BF),
            pltpu.VMEM((2, 16, 128), BF),
            pltpu.VMEM((2, 2, 16, 16, 128), BF),
            pltpu.VMEM((ROWS, D), BF),
            pltpu.VMEM((ROWS, D), BF),
            pltpu.VMEM((ROWS, D), BF),
            pltpu.VMEM((ROWS, D), BF),
            pltpu.VMEM((ROWS, D), F32),
            dma((4,)),
            pltpu.SemaphoreType.REGULAR((3,)),
            dma((2, N_G)), dma((2, N_G)),
            dma((2, N_G)), dma((2, N_G)),
            dma((2,)), dma((2,)),
            dma((5,)), dma((5,)),
            dma((2, 2, 3)), dma((2, 2, 3)),
            dma((2, 2, 3)), dma((2, 2, 3)),
            dma((2, n_z)), dma((2, n_z)),
            dma((2, NZ, 2)), dma((2,)),
        ],
        compiler_params=pltpu.CompilerParams(collective_id=0, has_side_effects=True, vmem_limit_bytes=50 * 2**20),
        name="layer",
    )(tokens, cotangent, valid, input_weight, output_weight)


def solution(mesh):
    placed = (
        P(("dp", "blk"), None),
        P(("dp", "blk")),
        P(("dp", "blk"), None),
        P("blk", None),
        P("blk", None),
    )
    return jax.shard_map(
        per_device,
        mesh=mesh,
        in_specs=placed,
        out_specs=(P(("dp", "blk"), None), P(("dp", "blk"), None), P("blk", None), P("blk", None)),
        check_vma=False,
    )
```

```python
import functools

import jax
import jax.numpy as jnp
from jax import lax
from jax.experimental import pallas as pl
from jax.experimental.pallas import tpu as pltpu
from jax.sharding import PartitionSpec as P

HEADS = 8
HEAD_SIZE = 64
CAPLEN = 32
EPSILON = 1e-06

MESH = pl.DeviceIdType.MESH
NX, NY, NZ = 4, 4, 16
ROWS = 256
D = 1024
HALF = 256
TILE = 128
BF = jnp.bfloat16
F32 = jnp.float32

GATHER = [(0, 1, 0), (0, 3, 0), (1, 0, 0), (0, 1, 1), (0, 3, 1), (1, 0, 1), (1, 1, 0), (1, 3, 0), (1, 1, 1), (1, 3, 1)]
GATHER += [(0, 2, 0), (0, 2, 1), (1, 2, 0), (1, 2, 1)]
N_G = len(GATHER)


def device(x, y, z, c):
    return {"dp": (x % 2) * NZ + z, "blk": y * 4 + (x // 2) * 2 + c}


def dot(a, b, ca, cb):
    return lax.dot_general(a, b, (((ca,), (cb,)), ((), ())), preferred_element_type=F32)


def kernel(
    tok_hbm, cot_hbm, lengths_ref, win_hbm, wout_hbm,
    lo_hbm, gt_hbm, gin_hbm, gout_hbm,
    lo_ref, gt_ref, gin_ref, gout_ref, lens, tok_ref, cot_ref, win_ref, wout_ref,
    stage, w, tok2, cot2, lens2, normed, normed_t, cot_t, inverse, proj, gatt, att, grads, probs,
    terms, first_in, first_sum, second_in, acc, z_in, red, fin, mixed_out, gn_out, mixed_in, gn_in, gn_own,
    l_sem, o_sem, ready, g_send, g_recv, h_send, h_recv, w_send, w_recv, s_send, s_recv, p_send, p_recv, q_send, q_recv, z_send, z_recv, f_send, f_recv,
):
    dp, blk = lax.axis_index("dp"), lax.axis_index("blk")
    xl, z = dp // NZ, dp % NZ
    y, xh, c = blk // 4, (blk // 2) % 2, blk % 2
    x = xh * 2 + xl
    sibling = device(x, y, z, 1 - c)

    loads = []
    for j, (src, dst) in enumerate(((win_hbm, win_ref), (wout_hbm, wout_ref), (tok_hbm, tok_ref), (cot_hbm, cot_ref))):
        cp = pltpu.make_async_copy(src, dst, l_sem.at[j])
        cp.start()
        loads.append(cp)

    def gather_to(cross, dy, dc):
        tx = 3 - x if cross else x
        return device(tx, (y + dy) % NY, z, (c + dc) % 2), (c + dc) % 2

    barrier = pltpu.get_barrier_semaphore()
    greet = [gather_to(*o)[0] for o in GATHER] + [sibling]
    greet += [device((x + d) % NX, y, z, c) for d in (1, 2, 3)]
    greet += [device(x, y, (z + d) % NZ, c) for d in (1, NZ - 1)]
    greet += [device(xh * 2 + 1 - xl, y, z, 1 - c)]
    for d in greet:
        pl.semaphore_signal(barrier, inc=1, device_id=d, device_id_type=MESH)

    def ready_signal(k):
        for d in (1 << k, NZ - (1 << k)):
            pl.semaphore_signal(ready.at[k], inc=1, device_id=device(x, y, (z + d) % NZ, c), device_id_type=MESH)

    def ready_wait(k):
        pl.semaphore_wait(ready.at[k], 2)

    def copy(src, dst, ss, rs, to):
        return pltpu.make_async_remote_copy(src_ref=src, dst_ref=dst, send_sem=ss, recv_sem=rs, device_id=to, device_id_type=MESH)

    caption = lax.broadcasted_iota(jnp.int32, (8, ROWS), 1) // CAPLEN
    held = jnp.zeros((8, ROWS), F32)
    for n in range(ROWS // CAPLEN):
        held = jnp.where(caption == n, lengths_ref[n].astype(F32), held)
    lens[...] = held

    loads[0].wait()
    loads[1].wait()
    for h in range(2):
        for i in range(2):
            for part in range(3):
                at = part * 2 * HALF + h * HALF + i * 128
                stage[h, i, :, part * 128 : (part + 1) * 128] = win_ref[:, at : at + 128]
            at = h * HALF + i * 128
            stage[h, i, :, 384:] = wout_ref[:, at : at + 128]
    my_rows = pl.ds(pl.multiple_of(blk * 64, 64), 64)
    for i in range(2):
        w[i, my_rows, :] = stage[c, i]

    def normalise(src, other, at):
        @pl.loop(0, 2)
        def _(i):
            rows = pl.ds(pl.multiple_of(i * 128, 128), 128)
            out = pl.ds(pl.multiple_of(at + i * 128, 128), 128)
            floats = src[rows, :].astype(F32)
            inv = lax.rsqrt(jnp.mean(floats * floats, axis=-1, keepdims=True) + EPSILON)
            inverse[out, :] = jnp.broadcast_to(inv, (128, 128))
            normed[out, :] = (floats * inv).astype(BF)

        @pl.loop(0, 4)
        def _(i):
            cols = pl.ds(pl.multiple_of(i * 256, 256), 256)
            normed_t[cols, at : at + ROWS] = normed[at : at + ROWS, cols].T
            cot_t[cols, at : at + ROWS] = other[:, cols].T

    pl.semaphore_wait(barrier, len(greet))
    ready_signal(0)

    shares = [
        copy(tok_ref, tok2, s_send.at[0], s_recv.at[0], sibling),
        copy(cot_ref, cot2, s_send.at[1], s_recv.at[1], sibling),
        copy(lens, lens2, s_send.at[2], s_recv.at[2], sibling),
    ]
    colour = (z + xl + xh) % 2
    half = pl.ds(pl.multiple_of(colour * 32, 32), 32)
    my_half = pl.ds(pl.multiple_of(blk * 64 + colour * 32, 32), 32)
    hand_to = [device(x, y, (z + 1) % NZ, c), device(x, y, (z + NZ - 1) % NZ, c), device(xh * 2 + 1 - xl, y, z, c)]

    def direct_start(i):
        started = []
        for j, o in enumerate(GATHER):
            to, h = gather_to(*o)
            started.append(copy(stage.at[h, i, half], w.at[i, my_half], g_send.at[i, j], g_recv.at[i, j], to))
        for cp in started:
            cp.start()
        return started

    def hand_start(i, j):
        cross, dy, dc = GATHER[j]
        block = (y + NY - dy) % NY * 4 + (1 - xh if cross else xh) * 2 + (c + dc) % 2
        rows = pl.ds(pl.multiple_of(block * 64 + colour * 32, 32), 32)
        cp = copy(w.at[i, rows], w.at[i, rows], h_send.at[i, j], h_recv.at[i, j], hand_to[j % 3])
        cp.start()
        return cp

    wides = [copy(stage.at[1 - c, i], w.at[i, my_rows], w_send.at[i], w_recv.at[i], sibling) for i in range(2)]
    direct0 = direct_start(0)
    loads[2].wait()
    loads[3].wait()
    shares[0].start()
    shares[1].start()
    shares[2].start()
    wides[0].start()
    wides[1].start()
    normalise(tok_ref, cot_ref, 0)
    ready_wait(0)
    ready_signal(1)
    hands0 = []
    for j in range(6):
        direct0[j].wait_recv()
        hands0.append(hand_start(0, j))
    direct1 = direct_start(1)
    for j in range(6, N_G):
        direct0[j].wait_recv()
        hands0.append(hand_start(0, j))
    for cp in shares:
        cp.wait()
    normalise(tok2, cot2, ROWS)
    ready_wait(1)
    ready_signal(2)

    def gather_end(i, hands):
        for cp in hands:
            cp.wait_recv()
        wides[i].wait_recv()

    key_at = lax.broadcasted_iota(jnp.int32, (TILE, 2 * TILE), 0)
    query_at = lax.broadcasted_iota(jnp.int32, (TILE, 2 * TILE), 1) % TILE
    causal = (key_at // CAPLEN == query_at // CAPLEN) & (key_at <= query_at)
    key_place = (key_at % CAPLEN).astype(F32)
    scale = HEAD_SIZE ** (-0.5)
    first_head = lax.broadcasted_iota(jnp.int32, (TILE, 128), 1) < HEAD_SIZE
    tiles = [(side, t) for side in range(2) for t in range(ROWS // TILE)]
    tile_rows = [slice(side * ROWS + t * TILE, side * ROWS + (t + 1) * TILE) for side, t in tiles]

    def stack(pair):
        zero = jnp.zeros_like(pair)
        return jnp.concatenate([jnp.where(first_head, pair, zero), jnp.where(first_head, zero, pair)], axis=0)

    def unstack(both):
        return jnp.where(first_head, both[:TILE], both[TILE:])

    def project(i):
        for r, src in enumerate((cot_ref, cot2)):
            own = slice(r * 256, (r + 1) * 256)
            proj[own, :] = dot(normed[own, :], w[i, :, :384], 1, 0).astype(BF)
            gatt[own, :] = dot(src[...], w[i, :, 384:], 1, 0).astype(BF)

    def attend(i):
        scores = [dot(proj[r, 128:256], stack(proj[r, :128]), 1, 1) for r in tile_rows]
        raised = []
        for (side, t), sc in zip(tiles, scores):
            real = (lens, lens2)[side][0:1, t * TILE : (t + 1) * TILE]
            allowed = causal & (key_place < jnp.concatenate([real, real], axis=1))
            raised.append(jnp.where(allowed, jnp.exp(sc * scale), 0.0))
        prob = [e / jnp.sum(e, axis=0, keepdims=True) for e in raised]
        for n, p in enumerate(prob):
            probs[n] = p
        rounded = [p.astype(BF) for p in prob]
        for r, p in zip(tile_rows, rounded):
            grads[i, r, 256:] = dot(p, stack(gatt[r, :]), 1, 0).astype(BF)
        for r, p in zip(tile_rows, rounded):
            att[i, r, :] = unstack(dot(p, proj[r, 256:], 0, 0)).astype(BF)

    def attend_back(i):
        grad_prob = [dot(proj[r, 256:], stack(gatt[r, :]), 1, 1) for r in tile_rows]
        grad_scores = []
        for n, gp in enumerate(grad_prob):
            p = probs[n]
            grad_scores.append((p * (gp - jnp.sum(p * gp, axis=0, keepdims=True)) * scale).astype(BF))
        for r, gs in zip(tile_rows, grad_scores):
            grads[i, r, 128:256] = dot(gs, stack(proj[r, :128]), 1, 0).astype(BF)
        for r, gs in zip(tile_rows, grad_scores):
            grads[i, r, :128] = unstack(dot(gs, proj[r, 128:256], 0, 0)).astype(BF)

    def products_values(i):
        @pl.loop(0, 4)
        def _(t):
            rows = pl.ds(pl.multiple_of(t * 256, 256), 256)
            terms[i, 2, t] = dot(normed_t[rows, :], grads[i, :, 256:], 1, 0).astype(BF).reshape(4, 64, 128)
            terms[i, 3, t] = dot(cot_t[rows, :], att[i], 1, 0).astype(BF).reshape(4, 64, 128)

    def products_scores(i):
        @pl.loop(0, 4)
        def _(t):
            rows = pl.ds(pl.multiple_of(t * 256, 256), 256)
            both = dot(normed_t[rows, :], grads[i, :, :256], 1, 0).astype(BF)
            terms[i, 0, t] = both[:, :128].reshape(4, 64, 128)
            terms[i, 1, t] = both[:, 128:].reshape(4, 64, 128)

    def first_start(i, groups):
        started = []
        for d in (1, 2, 3):
            tx, ty = (x + d) % NX, (y + d) % NY
            for g in groups:
                src = terms.at[i, g, ty] if g % 2 else terms.at[i, g, :, tx]
                to = device(x, ty, z, c) if g % 2 else device(tx, y, z, c)
                started.append(copy(src, first_in.at[i, g, d - 1], p_send.at[i, g, d - 1], p_recv.at[i, g, d - 1], to))
        for cp in started:
            cp.start()
        return started

    def first_end(i, groups, started):
        for cp in started:
            cp.wait()
        for g in groups:
            for n in range(4):
                total = (terms[i, g, y, n] if g % 2 else terms[i, g, n, x]).astype(F32)
                for d in range(3):
                    total = total + first_in[i, g, d, n].astype(F32)
                first_sum[i, g, n] = total.astype(BF)
        started = []
        for d in (1, 2, 3):
            tx, ty = (x + d) % NX, (y + d) % NY
            for g in groups:
                to = device(tx, y, z, c) if g % 2 else device(x, ty, z, c)
                started.append(copy(first_sum.at[i, g, tx if g % 2 else ty], second_in.at[i, g, d - 1], q_send.at[i, g, d - 1], q_recv.at[i, g, d - 1], to))
        for cp in started:
            cp.start()
        return started

    def second_end(i, started):
        for cp in started:
            cp.wait()
        for g in range(4):
            total = first_sum[i, g, x if g % 2 else y].astype(F32)
            for d in range(3):
                total = total + second_in[i, g, d].astype(F32)
            total = total.astype(BF)
            for n in range(4):
                acc[i, n * 4 + g] = total[n * 16 : (n + 1) * 16]
        started = []
        for dz in range(1, NZ):
            tz = (z + dz) % NZ
            started.append(copy(acc.at[i, tz], z_in.at[i, dz - 1], z_send.at[i, dz - 1], z_recv.at[i, dz - 1], device(x, y, tz, c)))
        for cp in started:
            cp.start()
        return started

    def line_end(i, started):
        for cp in started:
            cp.wait()
        total = acc[i, z].astype(F32)
        for j in range(NZ - 1):
            total = total + z_in[i, j].astype(F32)
        red[i] = total.astype(BF)
        started = []
        for dz in range(NZ):
            tz = (z + dz) % NZ
            for other in range(2):
                if dz or other:
                    tx = xh * 2 + (xl + other) % 2
                    started.append(copy(red.at[i], fin.at[i, c, z], f_send.at[i, dz, other], f_recv.at[i], device(tx, y, tz, xl)))
        for cp in started:
            cp.start()
        beside = copy(red.at[i], fin.at[i, c, z], f_send.at[i, 0, 0], f_recv.at[i], sibling)
        here = pltpu.make_async_copy(red.at[i], fin.at[i, c, z], f_recv.at[i])

        @pl.when(c != xl)
        def _():
            beside.start()

        @pl.when(c == xl)
        def _():
            here.start()

        return started, beside

    def back_end(i):
        pltpu.make_async_copy(fin.at[i], fin.at[i], f_recv.at[i]).wait()
        for h in range(2):
            for s in range(16):
                rows = slice(s // 4 * 16, (s // 4 + 1) * 16)
                part = s % 4
                at = h * HALF + i * 128
                value = fin[i, h, s].astype(F32)
                if part < 3:
                    gin_ref[rows, part * 512 + at : part * 512 + at + 128] = value
                else:
                    gout_ref[rows, at : at + 128] = value

    def back_sent(started, beside):
        for cp in started:
            cp.wait_send()

        @pl.when(c != xl)
        def _():
            beside.wait_send()

    values, score_groups = (2, 3), (0, 1)
    gather_end(0, hands0)
    project(0)
    hands1 = []
    for j in range(N_G):
        direct1[j].wait_recv()
        hands1.append(hand_start(1, j))
    attend(0)
    products_values(0)
    first0v = first_start(0, values)
    attend_back(0)
    products_scores(0)
    first0s = first_start(0, score_groups)
    gather_end(1, hands1)
    project(1)
    attend(1)
    products_values(1)
    first1v = first_start(1, values)
    second0v = first_end(0, values, first0v)
    attend_back(1)
    products_scores(1)
    first1s = first_start(1, score_groups)
    second0s = first_end(0, score_groups, first0s)
    ready_wait(2)

    def head_sums(rows, cols):
        mixed = dot(att[0, rows, :], w[0, cols, 384:], 1, 1) + dot(att[1, rows, :], w[1, cols, 384:], 1, 1)
        back = dot(grads[0, rows, :], w[0, cols, :384], 1, 1) + dot(grads[1, rows, :], w[1, cols, :384], 1, 1)
        return mixed, back

    @pl.loop(0, 4)
    def _(t):
        cols = pl.ds(pl.multiple_of(t * 256, 256), 256)
        mixed, back = head_sums(slice(ROWS, 2 * ROWS), cols)
        mixed_out[:, cols] = mixed.astype(BF)
        gn_out[:, cols] = back.astype(BF)

    backs = [
        copy(mixed_out, mixed_in, s_send.at[3], s_recv.at[3], sibling),
        copy(gn_out, gn_in, s_send.at[4], s_recv.at[4], sibling),
    ]
    for cp in backs:
        cp.start()
    second1v = first_end(1, values, first1v)
    line0 = second_end(0, second0v + second0s)

    @pl.loop(0, 4)
    def _(t):
        cols = pl.ds(pl.multiple_of(t * 256, 256), 256)
        mixed, back = head_sums(slice(0, ROWS), cols)
        lo_ref[:, cols] = (tok_ref[:, cols].astype(F32) + mixed).astype(BF)
        gn_own[:, cols] = back

    second1s = first_end(1, score_groups, first1s)
    line1 = second_end(1, second1v + second1s)
    back0 = line_end(0, line0)

    for cp in backs:
        cp.wait()

    @pl.loop(0, 4)
    def _(t):
        rows = pl.ds(pl.multiple_of(t * 64, 64), 64)
        floats = tok_ref[rows, :].astype(F32)
        inv = inverse[rows, 0:1]
        grad_normed = gn_own[rows, :] + gn_in[rows, :].astype(F32)
        mean = jnp.mean(grad_normed * floats, axis=-1, keepdims=True)
        gt_ref[rows, :] = (cot_ref[rows, :].astype(F32) + inv * grad_normed - floats * (inv * inv * inv * mean)).astype(BF)
        lo_ref[rows, :] = (lo_ref[rows, :].astype(F32) + mixed_in[rows, :].astype(F32)).astype(BF)

    outs = [
        pltpu.make_async_copy(lo_ref, lo_hbm, o_sem.at[0]),
        pltpu.make_async_copy(gt_ref, gt_hbm, o_sem.at[1]),
        pltpu.make_async_copy(gin_ref, gin_hbm, o_sem.at[2]),
        pltpu.make_async_copy(gout_ref, gout_hbm, o_sem.at[3]),
    ]
    outs[0].start()
    outs[1].start()
    back1 = line_end(1, line1)
    back_end(0)
    back_end(1)
    outs[2].start()
    outs[3].start()
    back_sent(*back0)
    back_sent(*back1)
    for cp in direct0 + direct1 + hands0 + hands1 + wides:
        cp.wait_send()
    for cp in outs:
        cp.wait()


def hand_over(*refs):
    sems = refs[-1]
    here = refs[8:12]
    loads = [pltpu.make_async_copy(src, mid, sems.at[0, j]) for j, (src, mid) in enumerate(zip(refs[:4], here))]
    stores = [pltpu.make_async_copy(mid, dst, sems.at[1, j]) for j, (mid, dst) in enumerate(zip(here, refs[4:8]))]
    for cp in loads:
        cp.start()
    for load, store in zip(loads, stores):
        load.wait()
        store.start()
    for cp in stores:
        cp.wait()


def per_device(tokens, lengths, cotangent, input_weight, output_weight):
    hbm, smem = pl.BlockSpec(memory_space=pl.ANY), pl.BlockSpec(memory_space=pltpu.SMEM)
    dma = pltpu.SemaphoreType.DMA
    n_z = NZ - 1
    shapes = (
        jax.ShapeDtypeStruct((ROWS, D), BF),
        jax.ShapeDtypeStruct((ROWS, D), BF),
        jax.ShapeDtypeStruct((64, 1536), F32),
        jax.ShapeDtypeStruct((64, 512), F32),
    )
    made = pl.pallas_call(
        kernel,
        out_shape=shapes,
        in_specs=[hbm, hbm, smem, hbm, hbm],
        out_specs=(hbm,) * 4,
        scratch_shapes=[
            pltpu.VMEM((ROWS, D), BF),
            pltpu.VMEM((ROWS, D), BF),
            pltpu.VMEM((64, 1536), F32),
            pltpu.VMEM((64, 512), F32),
            pltpu.VMEM((8, ROWS), F32),
            pltpu.VMEM((ROWS, D), BF),
            pltpu.VMEM((ROWS, D), BF),
            pltpu.VMEM((64, 1536), BF),
            pltpu.VMEM((64, 512), BF),
            pltpu.VMEM((2, 2, 64, 512), BF),
            pltpu.VMEM((2, D, 512), BF),
            pltpu.VMEM((ROWS, D), BF),
            pltpu.VMEM((ROWS, D), BF),
            pltpu.VMEM((8, ROWS), F32),
            pltpu.VMEM((2 * ROWS, D), BF),
            pltpu.VMEM((D, 2 * ROWS), BF),
            pltpu.VMEM((D, 2 * ROWS), BF),
            pltpu.VMEM((2 * ROWS, 128), F32),
            pltpu.VMEM((2 * ROWS, 384), BF),
            pltpu.VMEM((2 * ROWS, 128), BF),
            pltpu.VMEM((2, 2 * ROWS, 128), BF),
            pltpu.VMEM((2, 2 * ROWS, 384), BF),
            pltpu.VMEM((4, TILE, 2 * TILE), F32),
            pltpu.VMEM((2, 4, 4, 4, 64, 128), BF),
            pltpu.VMEM((2, 4, 3, 4, 64, 128), BF),
            pltpu.VMEM((2, 4, 4, 64, 128), BF),
            pltpu.VMEM((2, 4, 3, 64, 128), BF),
            pltpu.VMEM((2, 16, 16, 128), BF),
            pltpu.VMEM((2, n_z, 16, 128), BF),
            pltpu.VMEM((2, 16, 128), BF),
            pltpu.VMEM((2, 2, 16, 16, 128), BF),
            pltpu.VMEM((ROWS, D), BF),
            pltpu.VMEM((ROWS, D), BF),
            pltpu.VMEM((ROWS, D), BF),
            pltpu.VMEM((ROWS, D), BF),
            pltpu.VMEM((ROWS, D), F32),
            dma((4,)),
            dma((4,)),
            pltpu.SemaphoreType.REGULAR((3,)),
            dma((2, N_G)), dma((2, N_G)),
            dma((2, N_G)), dma((2, N_G)),
            dma((2,)), dma((2,)),
            dma((5,)), dma((5,)),
            dma((2, 4, 3)), dma((2, 4, 3)),
            dma((2, 4, 3)), dma((2, 4, 3)),
            dma((2, n_z)), dma((2, n_z)),
            dma((2, NZ, 2)), dma((2,)),
        ],
        compiler_params=pltpu.CompilerParams(collective_id=0, has_side_effects=True, vmem_limit_bytes=62 * 2**20),
        name="layer",
    )(tokens, cotangent, lengths, input_weight, output_weight)
    return pl.pallas_call(
        hand_over,
        out_shape=shapes,
        in_specs=[hbm] * 4,
        out_specs=(hbm,) * 4,
        scratch_shapes=[pltpu.VMEM(leaf.shape, leaf.dtype) for leaf in shapes] + [dma((2, 4))],
        compiler_params=pltpu.CompilerParams(vmem_limit_bytes=62 * 2**20),
        name="hand_over",
    )(*made)


def solution(mesh):
    placed = (
        P(("dp", "blk"), None),
        P(("dp", "blk")),
        P(("dp", "blk"), None),
        P("blk", None),
        P("blk", None),
    )
    return jax.shard_map(
        per_device,
        mesh=mesh,
        in_specs=placed,
        out_specs=(P(("dp", "blk"), None), P(("dp", "blk"), None), P("blk", None), P("blk", None)),
        check_vma=False,
    )
```

```python
import functools

import jax
import jax.numpy as jnp
from jax import lax
from jax.experimental import pallas as pl
from jax.experimental.pallas import tpu as pltpu
from jax.sharding import PartitionSpec as P

HEADS = 8
HEAD_SIZE = 64
CAPLEN = 32
EPSILON = 1e-06

MESH = pl.DeviceIdType.MESH
NX, NY, NZ = 4, 4, 16
ROWS = 256
D = 1024
HALF = 256
TILE = 128
BF = jnp.bfloat16
F32 = jnp.float32

GATHER = [(0, 1, 0), (0, 3, 0), (1, 0, 0), (0, 1, 1), (0, 3, 1), (1, 0, 1), (1, 1, 0), (1, 3, 0), (1, 1, 1), (1, 3, 1)]
GATHER += [(0, 2, 0), (0, 2, 1), (1, 2, 0), (1, 2, 1)]
N_G = len(GATHER)


def device(x, y, z, c):
    return {"dp": (x % 2) * NZ + z, "blk": y * 4 + (x // 2) * 2 + c}


def dot(a, b, ca, cb):
    return lax.dot_general(a, b, (((ca,), (cb,)), ((), ())), preferred_element_type=F32)


def kernel(
    tok_hbm, cot_hbm, lengths_ref, win_hbm, wout_hbm,
    lo_hbm, gt_hbm, gin_hbm, gout_hbm,
    lo_ref, gt_ref, gin_ref, gout_ref, lens, tok_ref, cot_ref, win_ref, wout_ref,
    stage, w, tok2, cot2, lens2, normed, normed_t, cot_t, inverse, proj, gatt, att, grads, probs,
    terms, first_in, first_sum, second_in, acc, z_in, red, fin, mixed_out, gn_out, mixed_in, gn_in, gn_own,
    l_sem, o_sem, ready, g_send, g_recv, h_send, h_recv, w_send, w_recv, s_send, s_recv, p_send, p_recv, q_send, q_recv, z_send, z_recv, f_send, f_recv,
):
    dp, blk = lax.axis_index("dp"), lax.axis_index("blk")
    xl, z = dp // NZ, dp % NZ
    y, xh, c = blk // 4, (blk // 2) % 2, blk % 2
    x = xh * 2 + xl
    sibling = device(x, y, z, 1 - c)

    loads = []
    for j, (src, dst) in enumerate(((win_hbm, win_ref), (wout_hbm, wout_ref), (tok_hbm, tok_ref), (cot_hbm, cot_ref))):
        cp = pltpu.make_async_copy(src, dst, l_sem.at[j])
        cp.start()
        loads.append(cp)

    def gather_to(cross, dy, dc):
        tx = 3 - x if cross else x
        return device(tx, (y + dy) % NY, z, (c + dc) % 2), (c + dc) % 2

    barrier = pltpu.get_barrier_semaphore()
    greet = [gather_to(*o)[0] for o in GATHER] + [sibling]
    greet += [device((x + d) % NX, y, z, c) for d in (1, 2, 3)]
    greet += [device(x, y, (z + d) % NZ, c) for d in (1, NZ - 1)]
    greet += [device(xh * 2 + 1 - xl, y, z, 1 - c)]
    for d in greet:
        pl.semaphore_signal(barrier, inc=1, device_id=d, device_id_type=MESH)

    def ready_signal(k):
        for d in (1 << k, NZ - (1 << k)):
            pl.semaphore_signal(ready.at[k], inc=1, device_id=device(x, y, (z + d) % NZ, c), device_id_type=MESH)

    def ready_wait(k):
        pl.semaphore_wait(ready.at[k], 2)

    def copy(src, dst, ss, rs, to):
        return pltpu.make_async_remote_copy(src_ref=src, dst_ref=dst, send_sem=ss, recv_sem=rs, device_id=to, device_id_type=MESH)

    caption = lax.broadcasted_iota(jnp.int32, (8, ROWS), 1) // CAPLEN
    held = jnp.zeros((8, ROWS), F32)
    for n in range(ROWS // CAPLEN):
        held = jnp.where(caption == n, lengths_ref[n].astype(F32), held)
    lens[...] = held

    loads[0].wait()
    loads[1].wait()
    for h in range(2):
        for i in range(2):
            for part in range(3):
                at = part * 2 * HALF + h * HALF + i * 128
                stage[h, i, :, part * 128 : (part + 1) * 128] = win_ref[:, at : at + 128]
            at = h * HALF + i * 128
            stage[h, i, :, 384:] = wout_ref[:, at : at + 128]
    my_rows = pl.ds(pl.multiple_of(blk * 64, 64), 64)
    for i in range(2):
        w[i, my_rows, :] = stage[c, i]

    def normalise(src, other, at):
        @pl.loop(0, 2)
        def _(i):
            rows = pl.ds(pl.multiple_of(i * 128, 128), 128)
            out = pl.ds(pl.multiple_of(at + i * 128, 128), 128)
            floats = src[rows, :].astype(F32)
            inv = lax.rsqrt(jnp.mean(floats * floats, axis=-1, keepdims=True) + EPSILON)
            inverse[out, :] = jnp.broadcast_to(inv, (128, 128))
            normed[out, :] = (floats * inv).astype(BF)

        @pl.loop(0, 4)
        def _(i):
            cols = pl.ds(pl.multiple_of(i * 256, 256), 256)
            normed_t[cols, at : at + ROWS] = normed[at : at + ROWS, cols].T
            cot_t[cols, at : at + ROWS] = other[:, cols].T

    pl.semaphore_wait(barrier, len(greet))
    ready_signal(0)

    shares = [
        copy(tok_ref, tok2, s_send.at[0], s_recv.at[0], sibling),
        copy(cot_ref, cot2, s_send.at[1], s_recv.at[1], sibling),
        copy(lens, lens2, s_send.at[2], s_recv.at[2], sibling),
    ]
    colour = (z + xl + xh) % 2
    half = pl.ds(pl.multiple_of(colour * 32, 32), 32)
    my_half = pl.ds(pl.multiple_of(blk * 64 + colour * 32, 32), 32)
    hand_to = [device(x, y, (z + 1) % NZ, c), device(x, y, (z + NZ - 1) % NZ, c), device(xh * 2 + 1 - xl, y, z, c)]

    def direct_start(i):
        started = []
        for j, o in enumerate(GATHER):
            to, h = gather_to(*o)
            started.append(copy(stage.at[h, i, half], w.at[i, my_half], g_send.at[i, j], g_recv.at[i, j], to))
        for cp in started:
            cp.start()
        return started

    def hand_start(i, j):
        cross, dy, dc = GATHER[j]
        block = (y + NY - dy) % NY * 4 + (1 - xh if cross else xh) * 2 + (c + dc) % 2
        rows = pl.ds(pl.multiple_of(block * 64 + colour * 32, 32), 32)
        cp = copy(w.at[i, rows], w.at[i, rows], h_send.at[i, j], h_recv.at[i, j], hand_to[j % 3])
        cp.start()
        return cp

    wides = [copy(stage.at[1 - c, i], w.at[i, my_rows], w_send.at[i], w_recv.at[i], sibling) for i in range(2)]
    direct0 = direct_start(0)
    loads[2].wait()
    loads[3].wait()
    shares[0].start()
    shares[1].start()
    shares[2].start()
    wides[0].start()
    wides[1].start()
    normalise(tok_ref, cot_ref, 0)
    ready_wait(0)
    ready_signal(1)
    hands0 = []
    for j in range(6):
        direct0[j].wait_recv()
        hands0.append(hand_start(0, j))
    direct1 = direct_start(1)
    for j in range(6, N_G):
        direct0[j].wait_recv()
        hands0.append(hand_start(0, j))
    for cp in shares:
        cp.wait()
    normalise(tok2, cot2, ROWS)
    ready_wait(1)
    ready_signal(2)

    def gather_end(i, hands):
        for cp in hands:
            cp.wait_recv()
        wides[i].wait_recv()

    key_at = lax.broadcasted_iota(jnp.int32, (TILE, 2 * TILE), 0)
    query_at = lax.broadcasted_iota(jnp.int32, (TILE, 2 * TILE), 1) % TILE
    causal = (key_at // CAPLEN == query_at // CAPLEN) & (key_at <= query_at)
    key_place = (key_at % CAPLEN).astype(F32)
    scale = HEAD_SIZE ** (-0.5)
    first_head = lax.broadcasted_iota(jnp.int32, (TILE, 128), 1) < HEAD_SIZE
    tiles = [(side, t) for side in range(2) for t in range(ROWS // TILE)]
    tile_rows = [slice(side * ROWS + t * TILE, side * ROWS + (t + 1) * TILE) for side, t in tiles]

    def stack(pair):
        zero = jnp.zeros_like(pair)
        return jnp.concatenate([jnp.where(first_head, pair, zero), jnp.where(first_head, zero, pair)], axis=0)

    def unstack(both):
        return jnp.where(first_head, both[:TILE], both[TILE:])

    def project(i):
        for r, src in enumerate((cot_ref, cot2)):
            own = slice(r * 256, (r + 1) * 256)
            proj[own, :] = dot(normed[own, :], w[i, :, :384], 1, 0).astype(BF)
            gatt[own, :] = dot(src[...], w[i, :, 384:], 1, 0).astype(BF)

    def attend(i):
        scores = [dot(proj[r, 128:256], stack(proj[r, :128]), 1, 1) for r in tile_rows]
        raised = []
        for (side, t), sc in zip(tiles, scores):
            real = (lens, lens2)[side][0:1, t * TILE : (t + 1) * TILE]
            allowed = causal & (key_place < jnp.concatenate([real, real], axis=1))
            raised.append(jnp.where(allowed, jnp.exp(sc * scale), 0.0))
        prob = [e * (1.0 / jnp.sum(e, axis=0, keepdims=True)) for e in raised]
        for n, p in enumerate(prob):
            probs[n] = p
        rounded = [p.astype(BF) for p in prob]
        for r, p in zip(tile_rows, rounded):
            grads[i, r, 256:] = dot(p, stack(gatt[r, :]), 1, 0).astype(BF)
        for r, p in zip(tile_rows, rounded):
            att[i, r, :] = unstack(dot(p, proj[r, 256:], 0, 0)).astype(BF)

    def attend_back(i):
        grad_prob = [dot(proj[r, 256:], stack(gatt[r, :]), 1, 1) for r in tile_rows]
        grad_scores = []
        for n, gp in enumerate(grad_prob):
            p = probs[n]
            grad_scores.append((p * (gp - jnp.sum(p * gp, axis=0, keepdims=True)) * scale).astype(BF))
        for r, gs in zip(tile_rows, grad_scores):
            grads[i, r, 128:256] = dot(gs, stack(proj[r, :128]), 1, 0).astype(BF)
        for r, gs in zip(tile_rows, grad_scores):
            grads[i, r, :128] = unstack(dot(gs, proj[r, 128:256], 0, 0)).astype(BF)

    def products_values(i):
        @pl.loop(0, 4)
        def _(t):
            rows = pl.ds(pl.multiple_of(t * 256, 256), 256)
            terms[i, 2, t] = dot(normed_t[rows, :], grads[i, :, 256:], 1, 0).astype(BF).reshape(4, 64, 128)
            terms[i, 3, t] = dot(cot_t[rows, :], att[i], 1, 0).astype(BF).reshape(4, 64, 128)

    def products_scores(i):
        @pl.loop(0, 4)
        def _(t):
            rows = pl.ds(pl.multiple_of(t * 256, 256), 256)
            both = dot(normed_t[rows, :], grads[i, :, :256], 1, 0).astype(BF)
            terms[i, 0, t] = both[:, :128].reshape(4, 64, 128)
            terms[i, 1, t] = both[:, 128:].reshape(4, 64, 128)

    def first_start(i, groups):
        started = []
        for d in (1, 2, 3):
            tx, ty = (x + d) % NX, (y + d) % NY
            for g in groups:
                src = terms.at[i, g, ty] if g % 2 else terms.at[i, g, :, tx]
                to = device(x, ty, z, c) if g % 2 else device(tx, y, z, c)
                started.append(copy(src, first_in.at[i, g, d - 1], p_send.at[i, g, d - 1], p_recv.at[i, g, d - 1], to))
        for cp in started:
            cp.start()
        return started

    def first_end(i, groups, started):
        for cp in started:
            cp.wait()
        for g in groups:
            for n in range(4):
                total = (terms[i, g, y, n] if g % 2 else terms[i, g, n, x]).astype(F32)
                for d in range(3):
                    total = total + first_in[i, g, d, n].astype(F32)
                first_sum[i, g, n] = total.astype(BF)
        started = []
        for d in (1, 2, 3):
            tx, ty = (x + d) % NX, (y + d) % NY
            for g in groups:
                to = device(tx, y, z, c) if g % 2 else device(x, ty, z, c)
                started.append(copy(first_sum.at[i, g, tx if g % 2 else ty], second_in.at[i, g, d - 1], q_send.at[i, g, d - 1], q_recv.at[i, g, d - 1], to))
        for cp in started:
            cp.start()
        return started

    my_part = (z % 4) // 2

    def line_copies(i, part):
        base = z - z % 4 + 2 * part
        far, near = [], []
        for q in range(4):
            for e in range(2):
                to = (base + 4 * q + e) % NZ
                k = 2 * q + e
                cp = copy(acc.at[i, to], z_in.at[i, z], z_send.at[i, part, k], z_recv.at[i], device(x, y, to, c))
                if q:
                    far.append(cp)
                else:
                    near.append((to, cp))
        return far, near

    def second_end(i, part, started):
        for cp in started:
            cp.wait()
        for g in (2 * part, 2 * part + 1):
            total = first_sum[i, g, x if g % 2 else y].astype(F32)
            for d in range(3):
                total = total + second_in[i, g, d].astype(F32)
            total = total.astype(BF)
            for n in range(4):
                acc[i, n * 4 + g] = total[n * 16 : (n + 1) * 16]
        far, near = line_copies(i, part)
        for cp in far:
            cp.start()
        for to, cp in near:
            @pl.when(to != z)
            def _():
                cp.start()

        @pl.when(my_part == part)
        def _():
            pltpu.make_async_copy(acc.at[i, z], z_in.at[i, z], z_recv.at[i]).start()

    def line_sent(i, part):
        far, near = line_copies(i, part)
        for cp in far:
            cp.wait_send()
        for to, cp in near:
            @pl.when(to != z)
            def _():
                cp.wait_send()

    def back_copies(i):
        copies = []
        for dz in range(NZ):
            tz = (z + dz) % NZ
            for other in range(2):
                if dz or other:
                    tx = xh * 2 + (xl + other) % 2
                    copies.append(copy(red.at[i], fin.at[i, c, z], f_send.at[i, dz, other], f_recv.at[i], device(tx, y, tz, xl)))
        return copies, copy(red.at[i], fin.at[i, c, z], f_send.at[i, 0, 0], f_recv.at[i], sibling)

    def line_end(i, part):
        @pl.when(my_part == part)
        def _():
            pltpu.make_async_copy(z_in.at[i], z_in.at[i], z_recv.at[i]).wait()
            total = z_in[i, 0].astype(F32)
            for j in range(1, NZ):
                total = total + z_in[i, j].astype(F32)
            red[i] = total.astype(BF)
            copies, beside = back_copies(i)
            for cp in copies:
                cp.start()

            @pl.when(c != xl)
            def _():
                beside.start()

            @pl.when(c == xl)
            def _():
                pltpu.make_async_copy(red.at[i], fin.at[i, c, z], f_recv.at[i]).start()

    def back_end(i):
        pltpu.make_async_copy(fin.at[i], fin.at[i], f_recv.at[i]).wait()
        for h in range(2):
            for s in range(16):
                rows = slice(s // 4 * 16, (s // 4 + 1) * 16)
                part = s % 4
                at = h * HALF + i * 128
                value = fin[i, h, s].astype(F32)
                if part < 3:
                    gin_ref[rows, part * 512 + at : part * 512 + at + 128] = value
                else:
                    gout_ref[rows, at : at + 128] = value

    def back_sent(i):
        copies, beside = back_copies(i)
        for cp in copies:
            cp.wait_send()

        @pl.when(c != xl)
        def _():
            beside.wait_send()

    values, score_groups = (2, 3), (0, 1)
    gather_end(0, hands0)
    project(0)
    hands1 = []
    for j in range(N_G):
        direct1[j].wait_recv()
        hands1.append(hand_start(1, j))
    attend(0)
    products_values(0)
    first0v = first_start(0, values)
    attend_back(0)
    products_scores(0)
    first0s = first_start(0, score_groups)
    gather_end(1, hands1)
    project(1)
    attend(1)
    products_values(1)
    first1v = first_start(1, values)
    second0v = first_end(0, values, first0v)
    attend_back(1)
    products_scores(1)
    first1s = first_start(1, score_groups)
    second0s = first_end(0, score_groups, first0s)
    ready_wait(2)
    second_end(0, 1, second0v)

    def head_sums(rows, cols):
        mixed = dot(att[0, rows, :], w[0, cols, 384:], 1, 1) + dot(att[1, rows, :], w[1, cols, 384:], 1, 1)
        back = dot(grads[0, rows, :], w[0, cols, :384], 1, 1) + dot(grads[1, rows, :], w[1, cols, :384], 1, 1)
        return mixed, back

    @pl.loop(0, 4)
    def _(t):
        cols = pl.ds(pl.multiple_of(t * 256, 256), 256)
        mixed, back = head_sums(slice(ROWS, 2 * ROWS), cols)
        mixed_out[:, cols] = mixed.astype(BF)
        gn_out[:, cols] = back.astype(BF)

    backs = [
        copy(mixed_out, mixed_in, s_send.at[3], s_recv.at[3], sibling),
        copy(gn_out, gn_in, s_send.at[4], s_recv.at[4], sibling),
    ]
    for cp in backs:
        cp.start()
    second1v = first_end(1, values, first1v)
    second_end(0, 0, second0s)
    second1s = first_end(1, score_groups, first1s)
    second_end(1, 1, second1v)

    @pl.loop(0, 4)
    def _(t):
        cols = pl.ds(pl.multiple_of(t * 256, 256), 256)
        mixed, back = head_sums(slice(0, ROWS), cols)
        lo_ref[:, cols] = (tok_ref[:, cols].astype(F32) + mixed).astype(BF)
        gn_own[:, cols] = back

    second_end(1, 0, second1s)
    line_end(0, 1)
    line_end(0, 0)
    line_end(1, 1)

    for cp in backs:
        cp.wait()

    @pl.loop(0, 4)
    def _(t):
        rows = pl.ds(pl.multiple_of(t * 64, 64), 64)
        floats = tok_ref[rows, :].astype(F32)
        inv = inverse[rows, 0:1]
        grad_normed = gn_own[rows, :] + gn_in[rows, :].astype(F32)
        mean = jnp.mean(grad_normed * floats, axis=-1, keepdims=True)
        gt_ref[rows, :] = (cot_ref[rows, :].astype(F32) + inv * grad_normed - floats * (inv * inv * inv * mean)).astype(BF)
        lo_ref[rows, :] = (lo_ref[rows, :].astype(F32) + mixed_in[rows, :].astype(F32)).astype(BF)

    outs = [
        pltpu.make_async_copy(lo_ref, lo_hbm, o_sem.at[0]),
        pltpu.make_async_copy(gt_ref, gt_hbm, o_sem.at[1]),
        pltpu.make_async_copy(gin_ref, gin_hbm, o_sem.at[2]),
        pltpu.make_async_copy(gout_ref, gout_hbm, o_sem.at[3]),
    ]
    outs[0].start()
    outs[1].start()
    line_end(1, 0)
    back_end(0)
    back_end(1)
    outs[2].start()
    outs[3].start()
    for i in range(2):
        line_sent(i, 0)
        line_sent(i, 1)
        back_sent(i)
    for cp in direct0 + direct1 + hands0 + hands1 + wides:
        cp.wait_send()
    for cp in outs:
        cp.wait()


def hand_over(*refs):
    sems = refs[-1]
    here = refs[8:12]
    loads = [pltpu.make_async_copy(src, mid, sems.at[0, j]) for j, (src, mid) in enumerate(zip(refs[:4], here))]
    stores = [pltpu.make_async_copy(mid, dst, sems.at[1, j]) for j, (mid, dst) in enumerate(zip(here, refs[4:8]))]
    for cp in loads:
        cp.start()
    for load, store in zip(loads, stores):
        load.wait()
        store.start()
    for cp in stores:
        cp.wait()


def per_device(tokens, lengths, cotangent, input_weight, output_weight):
    hbm, smem = pl.BlockSpec(memory_space=pl.ANY), pl.BlockSpec(memory_space=pltpu.SMEM)
    dma = pltpu.SemaphoreType.DMA
    shapes = (
        jax.ShapeDtypeStruct((ROWS, D), BF),
        jax.ShapeDtypeStruct((ROWS, D), BF),
        jax.ShapeDtypeStruct((64, 1536), F32),
        jax.ShapeDtypeStruct((64, 512), F32),
    )
    made = pl.pallas_call(
        kernel,
        out_shape=shapes,
        in_specs=[hbm, hbm, smem, hbm, hbm],
        out_specs=(hbm,) * 4,
        scratch_shapes=[
            pltpu.VMEM((ROWS, D), BF),
            pltpu.VMEM((ROWS, D), BF),
            pltpu.VMEM((64, 1536), F32),
            pltpu.VMEM((64, 512), F32),
            pltpu.VMEM((8, ROWS), F32),
            pltpu.VMEM((ROWS, D), BF),
            pltpu.VMEM((ROWS, D), BF),
            pltpu.VMEM((64, 1536), BF),
            pltpu.VMEM((64, 512), BF),
            pltpu.VMEM((2, 2, 64, 512), BF),
            pltpu.VMEM((2, D, 512), BF),
            pltpu.VMEM((ROWS, D), BF),
            pltpu.VMEM((ROWS, D), BF),
            pltpu.VMEM((8, ROWS), F32),
            pltpu.VMEM((2 * ROWS, D), BF),
            pltpu.VMEM((D, 2 * ROWS), BF),
            pltpu.VMEM((D, 2 * ROWS), BF),
            pltpu.VMEM((2 * ROWS, 128), F32),
            pltpu.VMEM((2 * ROWS, 384), BF),
            pltpu.VMEM((2 * ROWS, 128), BF),
            pltpu.VMEM((2, 2 * ROWS, 128), BF),
            pltpu.VMEM((2, 2 * ROWS, 384), BF),
            pltpu.VMEM((4, TILE, 2 * TILE), F32),
            pltpu.VMEM((2, 4, 4, 4, 64, 128), BF),
            pltpu.VMEM((2, 4, 3, 4, 64, 128), BF),
            pltpu.VMEM((2, 4, 4, 64, 128), BF),
            pltpu.VMEM((2, 4, 3, 64, 128), BF),
            pltpu.VMEM((2, 16, 16, 128), BF),
            pltpu.VMEM((2, NZ, 16, 128), BF),
            pltpu.VMEM((2, 16, 128), BF),
            pltpu.VMEM((2, 2, 16, 16, 128), BF),
            pltpu.VMEM((ROWS, D), BF),
            pltpu.VMEM((ROWS, D), BF),
            pltpu.VMEM((ROWS, D), BF),
            pltpu.VMEM((ROWS, D), BF),
            pltpu.VMEM((ROWS, D), F32),
            dma((4,)),
            dma((4,)),
            pltpu.SemaphoreType.REGULAR((3,)),
            dma((2, N_G)), dma((2, N_G)),
            dma((2, N_G)), dma((2, N_G)),
            dma((2,)), dma((2,)),
            dma((5,)), dma((5,)),
            dma((2, 4, 3)), dma((2, 4, 3)),
            dma((2, 4, 3)), dma((2, 4, 3)),
            dma((2, 2, 8)), dma((2,)),
            dma((2, NZ, 2)), dma((2,)),
        ],
        compiler_params=pltpu.CompilerParams(collective_id=0, has_side_effects=True, vmem_limit_bytes=62 * 2**20),
        name="layer",
    )(tokens, cotangent, lengths, input_weight, output_weight)
    return pl.pallas_call(
        hand_over,
        out_shape=shapes,
        in_specs=[hbm] * 4,
        out_specs=(hbm,) * 4,
        scratch_shapes=[pltpu.VMEM(leaf.shape, leaf.dtype) for leaf in shapes] + [dma((2, 4))],
        compiler_params=pltpu.CompilerParams(vmem_limit_bytes=62 * 2**20),
        name="hand_over",
    )(*made)


def solution(mesh):
    placed = (
        P(("dp", "blk"), None),
        P(("dp", "blk")),
        P(("dp", "blk"), None),
        P("blk", None),
        P("blk", None),
    )
    return jax.shard_map(
        per_device,
        mesh=mesh,
        in_specs=placed,
        out_specs=(P(("dp", "blk"), None), P(("dp", "blk"), None), P("blk", None), P("blk", None)),
        check_vma=False,
    )
```

```python
import functools

import jax
import jax.numpy as jnp
from jax import lax
from jax.experimental import pallas as pl
from jax.experimental.pallas import tpu as pltpu
from jax.sharding import PartitionSpec as P

HEADS = 8
HEAD_SIZE = 64
CAPLEN = 32
EPSILON = 1e-06

MESH = pl.DeviceIdType.MESH
NX, NY, NZ = 4, 4, 16
ROWS = 256
D = 1024
HALF = 256
TILE = 128
BF = jnp.bfloat16
F32 = jnp.float32

GATHER = [(0, 1, 0), (0, 3, 0), (1, 0, 0), (0, 1, 1), (0, 3, 1), (1, 0, 1), (1, 1, 0), (1, 3, 0), (1, 1, 1), (1, 3, 1)]
GATHER += [(0, 2, 0), (0, 2, 1), (1, 2, 0), (1, 2, 1)]
N_G = len(GATHER)


def device(x, y, z, c):
    return {"dp": (x % 2) * NZ + z, "blk": y * 4 + (x // 2) * 2 + c}


def dot(a, b, ca, cb):
    return lax.dot_general(a, b, (((ca,), (cb,)), ((), ())), preferred_element_type=F32)


def kernel(
    tok_hbm, cot_hbm, lengths_ref, win_hbm, wout_hbm,
    lo_hbm, gt_hbm, gin_hbm, gout_hbm,
    lo_ref, gt_ref, gin_ref, gout_ref, lens, tok_ref, cot_ref, win_ref, wout_ref,
    stage, w, tok2, cot2, lens2, normed, normed_t, cot_t, inverse, proj, gatt, att, grads, probs,
    terms, first_in, first_sum, second_in, acc, z_in, red, fin, mixed_out, gn_out, mixed_in, gn_in, gn_own,
    l_sem, o_sem, ready, g_send, g_recv, h_send, h_recv, w_send, w_recv, s_send, s_recv, p_send, p_recv, q_send, q_recv, z_send, z_recv, f_send, f_recv,
):
    dp, blk = lax.axis_index("dp"), lax.axis_index("blk")
    xl, z = dp // NZ, dp % NZ
    y, xh, c = blk // 4, (blk // 2) % 2, blk % 2
    x = xh * 2 + xl
    sibling = device(x, y, z, 1 - c)

    loads = []
    for j, (src, dst) in enumerate(((win_hbm, win_ref), (wout_hbm, wout_ref), (tok_hbm, tok_ref), (cot_hbm, cot_ref))):
        cp = pltpu.make_async_copy(src, dst, l_sem.at[j])
        cp.start()
        loads.append(cp)

    def gather_to(cross, dy, dc):
        tx = 3 - x if cross else x
        return device(tx, (y + dy) % NY, z, (c + dc) % 2), (c + dc) % 2

    barrier = pltpu.get_barrier_semaphore()
    greet = [gather_to(*o)[0] for o in GATHER] + [sibling]
    greet += [device((x + d) % NX, y, z, c) for d in (1, 2, 3)]
    greet += [device(x, y, (z + d) % NZ, c) for d in (1, NZ - 1)]
    greet += [device(xh * 2 + 1 - xl, y, z, 1 - c)]
    for d in greet:
        pl.semaphore_signal(barrier, inc=1, device_id=d, device_id_type=MESH)

    def ready_signal(k):
        for d in (1 << k, NZ - (1 << k)):
            pl.semaphore_signal(ready.at[k], inc=1, device_id=device(x, y, (z + d) % NZ, c), device_id_type=MESH)

    def ready_wait(k):
        pl.semaphore_wait(ready.at[k], 2)

    def copy(src, dst, ss, rs, to):
        return pltpu.make_async_remote_copy(src_ref=src, dst_ref=dst, send_sem=ss, recv_sem=rs, device_id=to, device_id_type=MESH)

    caption = lax.broadcasted_iota(jnp.int32, (8, ROWS), 1) // CAPLEN
    held = jnp.zeros((8, ROWS), F32)
    for n in range(ROWS // CAPLEN):
        held = jnp.where(caption == n, lengths_ref[n].astype(F32), held)
    lens[...] = held

    loads[0].wait()
    loads[1].wait()
    for h in range(2):
        for i in range(2):
            for part in range(3):
                at = part * 2 * HALF + h * HALF + i * 128
                stage[h, i, :, part * 128 : (part + 1) * 128] = win_ref[:, at : at + 128]
            at = h * HALF + i * 128
            stage[h, i, :, 384:] = wout_ref[:, at : at + 128]
    my_rows = pl.ds(pl.multiple_of(blk * 64, 64), 64)
    for i in range(2):
        w[i, my_rows, :] = stage[c, i]

    def normalise(src, other, at):
        @pl.loop(0, 2)
        def _(i):
            rows = pl.ds(pl.multiple_of(i * 128, 128), 128)
            out = pl.ds(pl.multiple_of(at + i * 128, 128), 128)
            floats = src[rows, :].astype(F32)
            inv = lax.rsqrt(jnp.mean(floats * floats, axis=-1, keepdims=True) + EPSILON)
            inverse[out, :] = jnp.broadcast_to(inv, (128, 128))
            normed[out, :] = (floats * inv).astype(BF)

        @pl.loop(0, 4)
        def _(i):
            cols = pl.ds(pl.multiple_of(i * 256, 256), 256)
            normed_t[cols, at : at + ROWS] = normed[at : at + ROWS, cols].T
            cot_t[cols, at : at + ROWS] = other[:, cols].T

    pl.semaphore_wait(barrier, len(greet))
    ready_signal(0)

    shares = [
        copy(tok_ref, tok2, s_send.at[0], s_recv.at[0], sibling),
        copy(cot_ref, cot2, s_send.at[1], s_recv.at[1], sibling),
        copy(lens, lens2, s_send.at[2], s_recv.at[2], sibling),
    ]
    colour = (z + xl + xh) % 2
    half = pl.ds(pl.multiple_of(colour * 32, 32), 32)
    my_half = pl.ds(pl.multiple_of(blk * 64 + colour * 32, 32), 32)
    hand_to = [device(x, y, (z + 1) % NZ, c), device(x, y, (z + NZ - 1) % NZ, c), device(xh * 2 + 1 - xl, y, z, c)]

    def direct_start(i):
        started = []
        for j, o in enumerate(GATHER):
            to, h = gather_to(*o)
            started.append(copy(stage.at[h, i, half], w.at[i, my_half], g_send.at[i, j], g_recv.at[i, j], to))
        for cp in started:
            cp.start()
        return started

    def hand_start(i, j):
        cross, dy, dc = GATHER[j]
        block = (y + NY - dy) % NY * 4 + (1 - xh if cross else xh) * 2 + (c + dc) % 2
        rows = pl.ds(pl.multiple_of(block * 64 + colour * 32, 32), 32)
        cp = copy(w.at[i, rows], w.at[i, rows], h_send.at[i, j], h_recv.at[i, j], hand_to[j % 3])
        cp.start()
        return cp

    wides = [copy(stage.at[1 - c, i], w.at[i, my_rows], w_send.at[i], w_recv.at[i], sibling) for i in range(2)]
    direct0 = direct_start(0)
    loads[2].wait()
    loads[3].wait()
    shares[0].start()
    shares[1].start()
    shares[2].start()
    wides[0].start()
    wides[1].start()
    normalise(tok_ref, cot_ref, 0)
    ready_wait(0)
    ready_signal(1)
    hands0 = []
    for j in range(6):
        direct0[j].wait_recv()
        hands0.append(hand_start(0, j))
    direct1 = direct_start(1)
    for cp in shares:
        cp.wait()
    normalise(tok2, cot2, ROWS)
    for j in range(6, N_G):
        direct0[j].wait_recv()
        hands0.append(hand_start(0, j))
    ready_wait(1)
    ready_signal(2)

    def gather_end(i, hands):
        for cp in hands:
            cp.wait_recv()
        wides[i].wait_recv()

    key_at = lax.broadcasted_iota(jnp.int32, (TILE, 2 * TILE), 0)
    query_at = lax.broadcasted_iota(jnp.int32, (TILE, 2 * TILE), 1) % TILE
    causal = (key_at // CAPLEN == query_at // CAPLEN) & (key_at <= query_at)
    key_place = (key_at % CAPLEN).astype(F32)
    scale = HEAD_SIZE ** (-0.5)
    first_head = lax.broadcasted_iota(jnp.int32, (TILE, 128), 1) < HEAD_SIZE
    tiles = [(side, t) for side in range(2) for t in range(ROWS // TILE)]
    tile_rows = [slice(side * ROWS + t * TILE, side * ROWS + (t + 1) * TILE) for side, t in tiles]

    def stack(pair):
        zero = jnp.zeros_like(pair)
        return jnp.concatenate([jnp.where(first_head, pair, zero), jnp.where(first_head, zero, pair)], axis=0)

    def unstack(both):
        return jnp.where(first_head, both[:TILE], both[TILE:])

    def project(i):
        for r, src in enumerate((cot_ref, cot2)):
            own = slice(r * 256, (r + 1) * 256)
            proj[own, :] = dot(normed[own, :], w[i, :, :384], 1, 0).astype(BF)
            gatt[own, :] = dot(src[...], w[i, :, 384:], 1, 0).astype(BF)

    def attend(i):
        scores = [dot(proj[r, 128:256], stack(proj[r, :128]), 1, 1) for r in tile_rows]
        raised = []
        for (side, t), sc in zip(tiles, scores):
            real = (lens, lens2)[side][0:1, t * TILE : (t + 1) * TILE]
            allowed = causal & (key_place < jnp.concatenate([real, real], axis=1))
            raised.append(jnp.where(allowed, jnp.exp(sc * scale), 0.0))
        prob = [e * (1.0 / jnp.sum(e, axis=0, keepdims=True)) for e in raised]
        for n, p in enumerate(prob):
            probs[n] = p
        rounded = [p.astype(BF) for p in prob]
        for r, p in zip(tile_rows, rounded):
            grads[i, r, 256:] = dot(p, stack(gatt[r, :]), 1, 0).astype(BF)
        for r, p in zip(tile_rows, rounded):
            att[i, r, :] = unstack(dot(p, proj[r, 256:], 0, 0)).astype(BF)

    def attend_back(i):
        grad_prob = [dot(proj[r, 256:], stack(gatt[r, :]), 1, 1) for r in tile_rows]
        grad_scores = []
        for n, gp in enumerate(grad_prob):
            p = probs[n]
            grad_scores.append((p * (gp - jnp.sum(p * gp, axis=0, keepdims=True)) * scale).astype(BF))
        for r, gs in zip(tile_rows, grad_scores):
            grads[i, r, 128:256] = dot(gs, stack(proj[r, :128]), 1, 0).astype(BF)
        for r, gs in zip(tile_rows, grad_scores):
            grads[i, r, :128] = unstack(dot(gs, proj[r, 128:256], 0, 0)).astype(BF)

    def products_values(i):
        @pl.loop(0, 4)
        def _(t):
            rows = pl.ds(pl.multiple_of(t * 256, 256), 256)
            terms[i, 2, t] = dot(normed_t[rows, :], grads[i, :, 256:], 1, 0).astype(BF).reshape(4, 64, 128)
            terms[i, 3, t] = dot(cot_t[rows, :], att[i], 1, 0).astype(BF).reshape(4, 64, 128)

    def products_scores(i):
        @pl.loop(0, 4)
        def _(t):
            rows = pl.ds(pl.multiple_of(t * 256, 256), 256)
            both = dot(normed_t[rows, :], grads[i, :, :256], 1, 0).astype(BF)
            terms[i, 0, t] = both[:, :128].reshape(4, 64, 128)
            terms[i, 1, t] = both[:, 128:].reshape(4, 64, 128)

    def first_start(i, groups):
        started = []
        for d in (1, 2, 3):
            tx, ty = (x + d) % NX, (y + d) % NY
            for g in groups:
                src = terms.at[i, g, ty] if g % 2 else terms.at[i, g, :, tx]
                to = device(x, ty, z, c) if g % 2 else device(tx, y, z, c)
                started.append(copy(src, first_in.at[i, g, d - 1], p_send.at[i, g, d - 1], p_recv.at[i, g, d - 1], to))
        for cp in started:
            cp.start()
        return started

    def first_end(i, groups, started):
        for cp in started:
            cp.wait()
        for g in groups:
            for n in range(4):
                total = (terms[i, g, y, n] if g % 2 else terms[i, g, n, x]).astype(F32)
                for d in range(3):
                    total = total + first_in[i, g, d, n].astype(F32)
                first_sum[i, g, n] = total.astype(BF)
        started = []
        for d in (1, 2, 3):
            tx, ty = (x + d) % NX, (y + d) % NY
            for g in groups:
                to = device(tx, y, z, c) if g % 2 else device(x, ty, z, c)
                started.append(copy(first_sum.at[i, g, tx if g % 2 else ty], second_in.at[i, g, d - 1], q_send.at[i, g, d - 1], q_recv.at[i, g, d - 1], to))
        for cp in started:
            cp.start()
        return started

    my_part = (z % 4) // 2

    def line_copies(i, part):
        base = z - z % 4 + 2 * part
        far, near = [], []
        for q in range(4):
            for e in range(2):
                to = (base + 4 * q + e) % NZ
                k = 2 * q + e
                cp = copy(acc.at[i, to], z_in.at[i, z], z_send.at[i, part, k], z_recv.at[i], device(x, y, to, c))
                if q:
                    far.append(cp)
                else:
                    near.append((to, cp))
        return far, near

    def second_end(i, part, started):
        for cp in started:
            cp.wait()
        for g in (2 * part, 2 * part + 1):
            total = first_sum[i, g, x if g % 2 else y].astype(F32)
            for d in range(3):
                total = total + second_in[i, g, d].astype(F32)
            total = total.astype(BF)
            for n in range(4):
                acc[i, n * 4 + g] = total[n * 16 : (n + 1) * 16]
        far, near = line_copies(i, part)
        for cp in far:
            cp.start()
        for to, cp in near:
            @pl.when(to != z)
            def _():
                cp.start()

        @pl.when(my_part == part)
        def _():
            pltpu.make_async_copy(acc.at[i, z], z_in.at[i, z], z_recv.at[i]).start()

    def line_sent(i, part):
        far, near = line_copies(i, part)
        for cp in far:
            cp.wait_send()
        for to, cp in near:
            @pl.when(to != z)
            def _():
                cp.wait_send()

    def back_copies(i):
        copies = []
        for dz in range(NZ):
            tz = (z + dz) % NZ
            for other in range(2):
                if dz or other:
                    tx = xh * 2 + (xl + other) % 2
                    copies.append(copy(red.at[i], fin.at[i, c, z], f_send.at[i, dz, other], f_recv.at[i], device(tx, y, tz, xl)))
        return copies, copy(red.at[i], fin.at[i, c, z], f_send.at[i, 0, 0], f_recv.at[i], sibling)

    def line_end(i, part):
        @pl.when(my_part == part)
        def _():
            pltpu.make_async_copy(z_in.at[i], z_in.at[i], z_recv.at[i]).wait()
            total = z_in[i, 0].astype(F32)
            for j in range(1, NZ):
                total = total + z_in[i, j].astype(F32)
            red[i] = total.astype(BF)
            copies, beside = back_copies(i)
            for cp in copies:
                cp.start()

            @pl.when(c != xl)
            def _():
                beside.start()

            @pl.when(c == xl)
            def _():
                pltpu.make_async_copy(red.at[i], fin.at[i, c, z], f_recv.at[i]).start()

    def back_end(i):
        pltpu.make_async_copy(fin.at[i], fin.at[i], f_recv.at[i]).wait()
        for h in range(2):
            for s in range(16):
                rows = slice(s // 4 * 16, (s // 4 + 1) * 16)
                part = s % 4
                at = h * HALF + i * 128
                value = fin[i, h, s].astype(F32)
                if part < 3:
                    gin_ref[rows, part * 512 + at : part * 512 + at + 128] = value
                else:
                    gout_ref[rows, at : at + 128] = value

    def back_sent(i):
        copies, beside = back_copies(i)
        for cp in copies:
            cp.wait_send()

        @pl.when(c != xl)
        def _():
            beside.wait_send()

    values, score_groups = (2, 3), (0, 1)
    gather_end(0, hands0)
    project(0)
    hands1 = []
    for j in range(8):
        direct1[j].wait_recv()
        hands1.append(hand_start(1, j))
    attend(0)
    for j in range(8, N_G):
        direct1[j].wait_recv()
        hands1.append(hand_start(1, j))
    products_values(0)
    first0v = first_start(0, values)
    attend_back(0)
    products_scores(0)
    first0s = first_start(0, score_groups)
    gather_end(1, hands1)
    project(1)
    attend(1)
    products_values(1)
    first1v = first_start(1, values)
    second0v = first_end(0, values, first0v)
    attend_back(1)
    products_scores(1)
    first1s = first_start(1, score_groups)
    second0s = first_end(0, score_groups, first0s)
    ready_wait(2)
    second_end(0, 1, second0v)

    def head_sums(rows, cols):
        mixed = dot(att[0, rows, :], w[0, cols, 384:], 1, 1) + dot(att[1, rows, :], w[1, cols, 384:], 1, 1)
        back = dot(grads[0, rows, :], w[0, cols, :384], 1, 1) + dot(grads[1, rows, :], w[1, cols, :384], 1, 1)
        return mixed, back

    @pl.loop(0, 4)
    def _(t):
        cols = pl.ds(pl.multiple_of(t * 256, 256), 256)
        mixed, back = head_sums(slice(ROWS, 2 * ROWS), cols)
        mixed_out[:, cols] = mixed.astype(BF)
        gn_out[:, cols] = back.astype(BF)

    backs = [
        copy(mixed_out, mixed_in, s_send.at[3], s_recv.at[3], sibling),
        copy(gn_out, gn_in, s_send.at[4], s_recv.at[4], sibling),
    ]
    for cp in backs:
        cp.start()
    second1v = first_end(1, values, first1v)
    second1s = first_end(1, score_groups, first1s)
    second_end(0, 0, second0s)
    second_end(1, 1, second1v)

    @pl.loop(0, 4)
    def _(t):
        cols = pl.ds(pl.multiple_of(t * 256, 256), 256)
        mixed, back = head_sums(slice(0, ROWS), cols)
        lo_ref[:, cols] = (tok_ref[:, cols].astype(F32) + mixed).astype(BF)
        gn_own[:, cols] = back

    second_end(1, 0, second1s)
    line_end(0, 1)
    line_end(0, 0)
    line_end(1, 1)

    for cp in backs:
        cp.wait()

    @pl.loop(0, 4)
    def _(t):
        rows = pl.ds(pl.multiple_of(t * 64, 64), 64)
        floats = tok_ref[rows, :].astype(F32)
        inv = inverse[rows, 0:1]
        grad_normed = gn_own[rows, :] + gn_in[rows, :].astype(F32)
        mean = jnp.mean(grad_normed * floats, axis=-1, keepdims=True)
        gt_ref[rows, :] = (cot_ref[rows, :].astype(F32) + inv * grad_normed - floats * (inv * inv * inv * mean)).astype(BF)
        lo_ref[rows, :] = (lo_ref[rows, :].astype(F32) + mixed_in[rows, :].astype(F32)).astype(BF)

    outs = [
        pltpu.make_async_copy(lo_ref, lo_hbm, o_sem.at[0]),
        pltpu.make_async_copy(gt_ref, gt_hbm, o_sem.at[1]),
        pltpu.make_async_copy(gout_ref, gout_hbm, o_sem.at[2]),
    ]
    for n in range(4):
        rows = pl.ds(n * 16, 16)
        outs.append(pltpu.make_async_copy(gin_ref.at[rows], gin_hbm.at[rows], o_sem.at[3 + n]))
    outs[0].start()
    outs[1].start()
    line_end(1, 0)
    back_end(0)
    back_end(1)
    for cp in outs[2:]:
        cp.start()
    for i in range(2):
        line_sent(i, 0)
        line_sent(i, 1)
        back_sent(i)
    for cp in direct0 + direct1 + hands0 + hands1 + wides:
        cp.wait_send()
    for cp in outs:
        cp.wait()


def hand_over(*refs):
    sems, here = refs[-1], refs[8:12]
    loads, stores = [], []
    for j, (src, mid, dst) in enumerate(zip(refs[:4], here, refs[4:8])):
        size = src.shape[0] // 4
        for n in range(4):
            rows = pl.ds(n * size, size)
            loads.append(pltpu.make_async_copy(src.at[rows], mid.at[rows], sems.at[0, j, n]))
            stores.append(pltpu.make_async_copy(mid.at[rows], dst.at[rows], sems.at[1, j, n]))
    for cp in loads:
        cp.start()
    for load, store in zip(loads, stores):
        load.wait()
        store.start()
    for cp in stores:
        cp.wait()


def per_device(tokens, lengths, cotangent, input_weight, output_weight):
    hbm, smem = pl.BlockSpec(memory_space=pl.ANY), pl.BlockSpec(memory_space=pltpu.SMEM)
    dma = pltpu.SemaphoreType.DMA
    shapes = (
        jax.ShapeDtypeStruct((ROWS, D), BF),
        jax.ShapeDtypeStruct((ROWS, D), BF),
        jax.ShapeDtypeStruct((64, 1536), F32),
        jax.ShapeDtypeStruct((64, 512), F32),
    )
    made = pl.pallas_call(
        kernel,
        out_shape=shapes,
        in_specs=[hbm, hbm, smem, hbm, hbm],
        out_specs=(hbm,) * 4,
        scratch_shapes=[
            pltpu.VMEM((ROWS, D), BF),
            pltpu.VMEM((ROWS, D), BF),
            pltpu.VMEM((64, 1536), F32),
            pltpu.VMEM((64, 512), F32),
            pltpu.VMEM((8, ROWS), F32),
            pltpu.VMEM((ROWS, D), BF),
            pltpu.VMEM((ROWS, D), BF),
            pltpu.VMEM((64, 1536), BF),
            pltpu.VMEM((64, 512), BF),
            pltpu.VMEM((2, 2, 64, 512), BF),
            pltpu.VMEM((2, D, 512), BF),
            pltpu.VMEM((ROWS, D), BF),
            pltpu.VMEM((ROWS, D), BF),
            pltpu.VMEM((8, ROWS), F32),
            pltpu.VMEM((2 * ROWS, D), BF),
            pltpu.VMEM((D, 2 * ROWS), BF),
            pltpu.VMEM((D, 2 * ROWS), BF),
            pltpu.VMEM((2 * ROWS, 128), F32),
            pltpu.VMEM((2 * ROWS, 384), BF),
            pltpu.VMEM((2 * ROWS, 128), BF),
            pltpu.VMEM((2, 2 * ROWS, 128), BF),
            pltpu.VMEM((2, 2 * ROWS, 384), BF),
            pltpu.VMEM((4, TILE, 2 * TILE), F32),
            pltpu.VMEM((2, 4, 4, 4, 64, 128), BF),
            pltpu.VMEM((2, 4, 3, 4, 64, 128), BF),
            pltpu.VMEM((2, 4, 4, 64, 128), BF),
            pltpu.VMEM((2, 4, 3, 64, 128), BF),
            pltpu.VMEM((2, 16, 16, 128), BF),
            pltpu.VMEM((2, NZ, 16, 128), BF),
            pltpu.VMEM((2, 16, 128), BF),
            pltpu.VMEM((2, 2, 16, 16, 128), BF),
            pltpu.VMEM((ROWS, D), BF),
            pltpu.VMEM((ROWS, D), BF),
            pltpu.VMEM((ROWS, D), BF),
            pltpu.VMEM((ROWS, D), BF),
            pltpu.VMEM((ROWS, D), F32),
            dma((4,)),
            dma((7,)),
            pltpu.SemaphoreType.REGULAR((3,)),
            dma((2, N_G)), dma((2, N_G)),
            dma((2, N_G)), dma((2, N_G)),
            dma((2,)), dma((2,)),
            dma((5,)), dma((5,)),
            dma((2, 4, 3)), dma((2, 4, 3)),
            dma((2, 4, 3)), dma((2, 4, 3)),
            dma((2, 2, 8)), dma((2,)),
            dma((2, NZ, 2)), dma((2,)),
        ],
        compiler_params=pltpu.CompilerParams(collective_id=0, has_side_effects=True, vmem_limit_bytes=62 * 2**20),
        name="layer",
    )(tokens, cotangent, lengths, input_weight, output_weight)
    return pl.pallas_call(
        hand_over,
        out_shape=shapes,
        in_specs=[hbm] * 4,
        out_specs=(hbm,) * 4,
        scratch_shapes=[pltpu.VMEM(leaf.shape, leaf.dtype) for leaf in shapes] + [dma((2, 4, 4))],
        compiler_params=pltpu.CompilerParams(vmem_limit_bytes=62 * 2**20),
        name="hand_over",
    )(*made)


def solution(mesh):
    placed = (
        P(("dp", "blk"), None),
        P(("dp", "blk")),
        P(("dp", "blk"), None),
        P("blk", None),
        P("blk", None),
    )
    return jax.shard_map(
        per_device,
        mesh=mesh,
        in_specs=placed,
        out_specs=(P(("dp", "blk"), None), P(("dp", "blk"), None), P("blk", None), P("blk", None)),
        check_vma=False,
    )
```

```python
import functools

import jax
import jax.numpy as jnp
from jax import lax
from jax.experimental import pallas as pl
from jax.experimental.pallas import tpu as pltpu
from jax.sharding import PartitionSpec as P

HEADS = 8
HEAD_SIZE = 64
CAPLEN = 32
EPSILON = 1e-06

MESH = pl.DeviceIdType.MESH
NX, NY, NZ = 4, 4, 16
ROWS = 256
D = 1024
HALF = 256
TILE = 128
BF = jnp.bfloat16
F32 = jnp.float32

GATHER = [(0, 1, 0), (0, 3, 0), (1, 0, 0), (0, 1, 1), (0, 3, 1), (1, 0, 1), (1, 1, 0), (1, 3, 0), (1, 1, 1), (1, 3, 1)]
GATHER += [(0, 2, 0), (0, 2, 1), (1, 2, 0), (1, 2, 1)]
N_G = len(GATHER)


def device(x, y, z, c):
    return {"dp": (x % 2) * NZ + z, "blk": y * 4 + (x // 2) * 2 + c}


def dot(a, b, ca, cb):
    return lax.dot_general(a, b, (((ca,), (cb,)), ((), ())), preferred_element_type=F32)


def kernel(
    tok_hbm, cot_hbm, lengths_ref, win_hbm, wout_hbm,
    lo_hbm, gt_hbm, gin_hbm, gout_hbm,
    lo_ref, gt_ref, gin_ref, gout_ref, lens, tok_ref, cot_ref, win_ref, wout_ref,
    stage, w, tok2, cot2, lens2, normed, normed_t, cot_t, inverse, proj, gatt, att, grads, probs,
    terms, first_in, first_sum, second_in, acc, z_in, red, fin, mixed_out, gn_out, mixed_in, gn_in, gn_own,
    l_sem, o_sem, ready, g_send, g_recv, h_send, h_recv, w_send, w_recv, s_send, s_recv, p_send, p_recv, q_send, q_recv, z_send, z_recv, f_send, f_recv,
):
    dp, blk = lax.axis_index("dp"), lax.axis_index("blk")
    xl, z = dp // NZ, dp % NZ
    y, xh, c = blk // 4, (blk // 2) % 2, blk % 2
    x = xh * 2 + xl
    sibling = device(x, y, z, 1 - c)

    loads = []
    for j, (src, dst) in enumerate(((win_hbm, win_ref), (wout_hbm, wout_ref), (tok_hbm, tok_ref), (cot_hbm, cot_ref))):
        cp = pltpu.make_async_copy(src, dst, l_sem.at[j])
        cp.start()
        loads.append(cp)

    def gather_to(cross, dy, dc):
        tx = 3 - x if cross else x
        return device(tx, (y + dy) % NY, z, (c + dc) % 2), (c + dc) % 2

    barrier = pltpu.get_barrier_semaphore()
    greet = [gather_to(*o)[0] for o in GATHER] + [sibling]
    greet += [device((x + d) % NX, y, z, c) for d in (1, 2, 3)]
    greet += [device(x, y, (z + d) % NZ, c) for d in (1, NZ - 1)]
    greet += [device(xh * 2 + 1 - xl, y, z, 1 - c)]
    for d in greet:
        pl.semaphore_signal(barrier, inc=1, device_id=d, device_id_type=MESH)

    def ready_signal(k):
        for d in (1 << k, NZ - (1 << k)):
            pl.semaphore_signal(ready.at[k], inc=1, device_id=device(x, y, (z + d) % NZ, c), device_id_type=MESH)

    def ready_wait(k):
        pl.semaphore_wait(ready.at[k], 2)

    def copy(src, dst, ss, rs, to):
        return pltpu.make_async_remote_copy(src_ref=src, dst_ref=dst, send_sem=ss, recv_sem=rs, device_id=to, device_id_type=MESH)

    caption = lax.broadcasted_iota(jnp.int32, (8, ROWS), 1) // CAPLEN
    held = jnp.zeros((8, ROWS), F32)
    for n in range(ROWS // CAPLEN):
        held = jnp.where(caption == n, lengths_ref[n].astype(F32), held)
    lens[...] = held

    loads[0].wait()
    loads[1].wait()
    for h in range(2):
        for i in range(2):
            for part in range(3):
                at = part * 2 * HALF + h * HALF + i * 128
                stage[h, i, :, part * 128 : (part + 1) * 128] = win_ref[:, at : at + 128]
            at = h * HALF + i * 128
            stage[h, i, :, 384:] = wout_ref[:, at : at + 128]
    my_rows = pl.ds(pl.multiple_of(blk * 64, 64), 64)
    for i in range(2):
        w[i, my_rows, :] = stage[c, i]

    def normalise(src, other, at):
        @pl.loop(0, 2)
        def _(i):
            rows = pl.ds(pl.multiple_of(i * 128, 128), 128)
            out = pl.ds(pl.multiple_of(at + i * 128, 128), 128)
            floats = src[rows, :].astype(F32)
            inv = lax.rsqrt(jnp.mean(floats * floats, axis=-1, keepdims=True) + EPSILON)
            inverse[out, :] = jnp.broadcast_to(inv, (128, 128))
            normed[out, :] = (floats * inv).astype(BF)

        @pl.loop(0, 4)
        def _(i):
            cols = pl.ds(pl.multiple_of(i * 256, 256), 256)
            normed_t[cols, at : at + ROWS] = normed[at : at + ROWS, cols].T
            cot_t[cols, at : at + ROWS] = other[:, cols].T

    pl.semaphore_wait(barrier, len(greet))
    ready_signal(0)

    shares = [
        copy(tok_ref, tok2, s_send.at[0], s_recv.at[0], sibling),
        copy(cot_ref, cot2, s_send.at[1], s_recv.at[1], sibling),
        copy(lens, lens2, s_send.at[2], s_recv.at[2], sibling),
    ]
    colour = (z + xl + xh) % 2
    half = pl.ds(pl.multiple_of(colour * 32, 32), 32)
    my_half = pl.ds(pl.multiple_of(blk * 64 + colour * 32, 32), 32)
    hand_to = [device(x, y, (z + 1) % NZ, c), device(x, y, (z + NZ - 1) % NZ, c), device(xh * 2 + 1 - xl, y, z, c)]

    def direct_start(i):
        started = []
        for j, o in enumerate(GATHER):
            to, h = gather_to(*o)
            started.append(copy(stage.at[h, i, half], w.at[i, my_half], g_send.at[i, j], g_recv.at[i, j], to))
        for cp in started:
            cp.start()
        return started

    def hand_start(i, j):
        cross, dy, dc = GATHER[j]
        block = (y + NY - dy) % NY * 4 + (1 - xh if cross else xh) * 2 + (c + dc) % 2
        rows = pl.ds(pl.multiple_of(block * 64 + colour * 32, 32), 32)
        cp = copy(w.at[i, rows], w.at[i, rows], h_send.at[i, j], h_recv.at[i, j], hand_to[j % 3])
        cp.start()
        return cp

    wides = [copy(stage.at[1 - c, i], w.at[i, my_rows], w_send.at[i], w_recv.at[i], sibling) for i in range(2)]
    direct0 = direct_start(0)
    loads[2].wait()
    loads[3].wait()
    shares[0].start()
    shares[1].start()
    shares[2].start()
    wides[0].start()
    wides[1].start()
    normalise(tok_ref, cot_ref, 0)
    ready_wait(0)
    ready_signal(1)
    hands0 = []
    for j in range(6):
        direct0[j].wait_recv()
        hands0.append(hand_start(0, j))
    direct1 = direct_start(1)
    for cp in shares:
        cp.wait()
    normalise(tok2, cot2, ROWS)
    for j in range(6, N_G):
        direct0[j].wait_recv()
        hands0.append(hand_start(0, j))
    ready_wait(1)
    ready_signal(2)

    def gather_end(i, hands):
        for cp in hands:
            cp.wait_recv()
        wides[i].wait_recv()

    key_at = lax.broadcasted_iota(jnp.int32, (TILE, 2 * TILE), 0)
    query_at = lax.broadcasted_iota(jnp.int32, (TILE, 2 * TILE), 1) % TILE
    causal = (key_at // CAPLEN == query_at // CAPLEN) & (key_at <= query_at)
    key_place = (key_at % CAPLEN).astype(F32)
    scale = HEAD_SIZE ** (-0.5)
    first_head = lax.broadcasted_iota(jnp.int32, (TILE, 128), 1) < HEAD_SIZE
    tiles = [(side, t) for side in range(2) for t in range(ROWS // TILE)]
    tile_rows = [slice(side * ROWS + t * TILE, side * ROWS + (t + 1) * TILE) for side, t in tiles]

    def stack(pair):
        zero = jnp.zeros_like(pair)
        return jnp.concatenate([jnp.where(first_head, pair, zero), jnp.where(first_head, zero, pair)], axis=0)

    def unstack(both):
        return jnp.where(first_head, both[:TILE], both[TILE:])

    def project(i):
        proj[...] = dot(normed[...], w[i, :, :384], 1, 0).astype(BF)
        for r, src in enumerate((cot_ref, cot2)):
            own = slice(r * 256, (r + 1) * 256)
            gatt[own, :] = dot(src[...], w[i, :, 384:], 1, 0).astype(BF)

    def attend(i):
        scores = [dot(proj[r, 128:256], stack(proj[r, :128]), 1, 1) for r in tile_rows]
        raised = []
        for (side, t), sc in zip(tiles, scores):
            real = (lens, lens2)[side][0:1, t * TILE : (t + 1) * TILE]
            allowed = causal & (key_place < jnp.concatenate([real, real], axis=1))
            raised.append(jnp.where(allowed, jnp.exp(sc * scale), 0.0))
        prob = [e * (1.0 / jnp.sum(e, axis=0, keepdims=True)) for e in raised]
        for n, p in enumerate(prob):
            probs[n] = p
        rounded = [p.astype(BF) for p in prob]
        for r, p in zip(tile_rows, rounded):
            grads[i, r, 256:] = dot(p, stack(gatt[r, :]), 1, 0).astype(BF)
        for r, p in zip(tile_rows, rounded):
            att[i, r, :] = unstack(dot(p, proj[r, 256:], 0, 0)).astype(BF)

    def attend_back(i):
        grad_prob = [dot(proj[r, 256:], stack(gatt[r, :]), 1, 1) for r in tile_rows]
        grad_scores = []
        for n, gp in enumerate(grad_prob):
            p = probs[n]
            grad_scores.append((p * (gp - jnp.sum(p * gp, axis=0, keepdims=True)) * scale).astype(BF))
        for r, gs in zip(tile_rows, grad_scores):
            grads[i, r, 128:256] = dot(gs, stack(proj[r, :128]), 1, 0).astype(BF)
        for r, gs in zip(tile_rows, grad_scores):
            grads[i, r, :128] = unstack(dot(gs, proj[r, 128:256], 0, 0)).astype(BF)

    def products_values(i):
        for t in range(2):
            rows = slice(t * 512, (t + 1) * 512)
            terms[i, 2, 2 * t : 2 * t + 2] = dot(normed_t[rows, :], grads[i, :, 256:], 1, 0).astype(BF).reshape(2, 4, 64, 128)
            terms[i, 3, 2 * t : 2 * t + 2] = dot(cot_t[rows, :], att[i], 1, 0).astype(BF).reshape(2, 4, 64, 128)

    def products_scores(i):
        for t in range(2):
            rows = slice(t * 512, (t + 1) * 512)
            both = dot(normed_t[rows, :], grads[i, :, :256], 1, 0).astype(BF)
            terms[i, 0, 2 * t : 2 * t + 2] = both[:, :128].reshape(2, 4, 64, 128)
            terms[i, 1, 2 * t : 2 * t + 2] = both[:, 128:].reshape(2, 4, 64, 128)

    def first_start(i, groups):
        started = []
        for d in (2, 1, 3):
            tx, ty = (x + d) % NX, (y + d) % NY
            for g in groups:
                src = terms.at[i, g, ty] if g % 2 else terms.at[i, g, :, tx]
                to = device(x, ty, z, c) if g % 2 else device(tx, y, z, c)
                started.append(copy(src, first_in.at[i, g, d - 1], p_send.at[i, g, d - 1], p_recv.at[i, g, d - 1], to))
        for cp in started:
            cp.start()
        return started

    def first_end(i, groups, started):
        for cp in started:
            cp.wait()
        for g in groups:
            for n in range(4):
                total = (terms[i, g, y, n] if g % 2 else terms[i, g, n, x]).astype(F32)
                for d in range(3):
                    total = total + first_in[i, g, d, n].astype(F32)
                first_sum[i, g, n] = total.astype(BF)
        started = []
        for d in (2, 1, 3):
            tx, ty = (x + d) % NX, (y + d) % NY
            for g in groups:
                to = device(tx, y, z, c) if g % 2 else device(x, ty, z, c)
                started.append(copy(first_sum.at[i, g, tx if g % 2 else ty], second_in.at[i, g, d - 1], q_send.at[i, g, d - 1], q_recv.at[i, g, d - 1], to))
        for cp in started:
            cp.start()
        return started

    my_part = (z % 4) // 2

    def line_copies(i, part):
        base = z - z % 4 + 2 * part
        far, near = [], []
        for q in (2, 1, 3, 0):
            for e in range(2):
                to = (base + 4 * q + e) % NZ
                k = 2 * q + e
                cp = copy(acc.at[i, to], z_in.at[i, z], z_send.at[i, part, k], z_recv.at[i], device(x, y, to, c))
                if q:
                    far.append(cp)
                else:
                    near.append((to, cp))
        return far, near

    def second_end(i, part, started):
        for cp in started:
            cp.wait()
        for g in (2 * part, 2 * part + 1):
            total = first_sum[i, g, x if g % 2 else y].astype(F32)
            for d in range(3):
                total = total + second_in[i, g, d].astype(F32)
            total = total.astype(BF)
            for n in range(4):
                acc[i, n * 4 + g] = total[n * 16 : (n + 1) * 16]
        far, near = line_copies(i, part)
        for cp in far:
            cp.start()
        for to, cp in near:
            @pl.when(to != z)
            def _():
                cp.start()

        @pl.when(my_part == part)
        def _():
            pltpu.make_async_copy(acc.at[i, z], z_in.at[i, z], z_recv.at[i]).start()

    def line_sent(i, part):
        far, near = line_copies(i, part)
        for cp in far:
            cp.wait_send()
        for to, cp in near:
            @pl.when(to != z)
            def _():
                cp.wait_send()

    def back_copies(i):
        copies = []
        for dz in sorted(range(NZ), key=lambda d: -min(d, NZ - d)):
            tz = (z + dz) % NZ
            for other in range(2):
                if dz or other:
                    tx = xh * 2 + (xl + other) % 2
                    copies.append(copy(red.at[i], fin.at[i, c, z], f_send.at[i, dz, other], f_recv.at[i], device(tx, y, tz, xl)))
        return copies, copy(red.at[i], fin.at[i, c, z], f_send.at[i, 0, 0], f_recv.at[i], sibling)

    def line_end(i, part):
        @pl.when(my_part == part)
        def _():
            pltpu.make_async_copy(z_in.at[i], z_in.at[i], z_recv.at[i]).wait()
            total = z_in[i, 0].astype(F32)
            for j in range(1, NZ):
                total = total + z_in[i, j].astype(F32)
            red[i] = total.astype(BF)
            copies, beside = back_copies(i)
            for cp in copies:
                cp.start()

            @pl.when(c != xl)
            def _():
                beside.start()

            @pl.when(c == xl)
            def _():
                pltpu.make_async_copy(red.at[i], fin.at[i, c, z], f_recv.at[i]).start()

    def back_end(i):
        pltpu.make_async_copy(fin.at[i], fin.at[i], f_recv.at[i]).wait()
        for h in range(2):
            for s in range(16):
                rows = slice(s // 4 * 16, (s // 4 + 1) * 16)
                part = s % 4
                at = h * HALF + i * 128
                value = fin[i, h, s].astype(F32)
                if part < 3:
                    gin_ref[rows, part * 512 + at : part * 512 + at + 128] = value
                else:
                    gout_ref[rows, at : at + 128] = value

    def back_sent(i):
        copies, beside = back_copies(i)
        for cp in copies:
            cp.wait_send()

        @pl.when(c != xl)
        def _():
            beside.wait_send()

    values, score_groups = (2, 3), (0, 1)
    gather_end(0, hands0)
    project(0)
    hands1 = []
    for j in range(8):
        direct1[j].wait_recv()
        hands1.append(hand_start(1, j))
    attend(0)
    for j in range(8, N_G):
        direct1[j].wait_recv()
        hands1.append(hand_start(1, j))
    products_values(0)
    first0v = first_start(0, values)
    attend_back(0)
    products_scores(0)
    first0s = first_start(0, score_groups)
    gather_end(1, hands1)
    project(1)
    attend(1)
    products_values(1)
    first1v = first_start(1, values)
    second0v = first_end(0, values, first0v)
    attend_back(1)
    products_scores(1)
    first1s = first_start(1, score_groups)
    second0s = first_end(0, score_groups, first0s)
    ready_wait(2)
    second_end(0, 1, second0v)

    def head_sums(rows, cols):
        mixed = dot(att[0, rows, :], w[0, cols, 384:], 1, 1) + dot(att[1, rows, :], w[1, cols, 384:], 1, 1)
        back = dot(grads[0, rows, :], w[0, cols, :384], 1, 1) + dot(grads[1, rows, :], w[1, cols, :384], 1, 1)
        return mixed, back

    @pl.loop(0, 4)
    def _(t):
        cols = pl.ds(pl.multiple_of(t * 256, 256), 256)
        mixed, back = head_sums(slice(ROWS, 2 * ROWS), cols)
        mixed_out[:, cols] = mixed.astype(BF)
        gn_out[:, cols] = back.astype(BF)

    backs = [
        copy(mixed_out, mixed_in, s_send.at[3], s_recv.at[3], sibling),
        copy(gn_out, gn_in, s_send.at[4], s_recv.at[4], sibling),
    ]
    for cp in backs:
        cp.start()
    second1v = first_end(1, values, first1v)
    second1s = first_end(1, score_groups, first1s)
    second_end(0, 0, second0s)
    second_end(1, 1, second1v)

    @pl.loop(0, 4)
    def _(t):
        cols = pl.ds(pl.multiple_of(t * 256, 256), 256)
        mixed, back = head_sums(slice(0, ROWS), cols)
        lo_ref[:, cols] = (tok_ref[:, cols].astype(F32) + mixed).astype(BF)
        gn_own[:, cols] = back

    second_end(1, 0, second1s)
    line_end(0, 1)
    line_end(0, 0)
    line_end(1, 1)

    for cp in backs:
        cp.wait()

    @pl.loop(0, 4)
    def _(t):
        rows = pl.ds(pl.multiple_of(t * 64, 64), 64)
        floats = tok_ref[rows, :].astype(F32)
        inv = inverse[rows, 0:1]
        grad_normed = gn_own[rows, :] + gn_in[rows, :].astype(F32)
        mean = jnp.mean(grad_normed * floats, axis=-1, keepdims=True)
        gt_ref[rows, :] = (cot_ref[rows, :].astype(F32) + inv * grad_normed - floats * (inv * inv * inv * mean)).astype(BF)
        lo_ref[rows, :] = (lo_ref[rows, :].astype(F32) + mixed_in[rows, :].astype(F32)).astype(BF)

    outs = [
        pltpu.make_async_copy(lo_ref, lo_hbm, o_sem.at[0]),
        pltpu.make_async_copy(gt_ref, gt_hbm, o_sem.at[1]),
        pltpu.make_async_copy(gout_ref, gout_hbm, o_sem.at[2]),
    ]
    for n in range(4):
        rows = pl.ds(n * 16, 16)
        outs.append(pltpu.make_async_copy(gin_ref.at[rows], gin_hbm.at[rows], o_sem.at[3 + n]))
    outs[0].start()
    outs[1].start()
    line_end(1, 0)
    back_end(0)
    back_end(1)
    for cp in outs[2:]:
        cp.start()
    for i in range(2):
        line_sent(i, 0)
        line_sent(i, 1)
        back_sent(i)
    for cp in direct0 + direct1 + hands0 + hands1 + wides:
        cp.wait_send()
    for cp in outs:
        cp.wait()


def hand_over(*refs):
    sems, here = refs[-1], refs[8:12]
    loads, stores = [], []
    for j, (src, mid, dst) in enumerate(zip(refs[:4], here, refs[4:8])):
        size = src.shape[0] // 4
        for n in range(4):
            rows = pl.ds(n * size, size)
            loads.append(pltpu.make_async_copy(src.at[rows], mid.at[rows], sems.at[0, j, n]))
            stores.append(pltpu.make_async_copy(mid.at[rows], dst.at[rows], sems.at[1, j, n]))
    for cp in loads:
        cp.start()
    for load, store in zip(loads, stores):
        load.wait()
        store.start()
    for cp in stores:
        cp.wait()


def per_device(tokens, lengths, cotangent, input_weight, output_weight):
    hbm, smem = pl.BlockSpec(memory_space=pl.ANY), pl.BlockSpec(memory_space=pltpu.SMEM)
    dma = pltpu.SemaphoreType.DMA
    shapes = (
        jax.ShapeDtypeStruct((ROWS, D), BF),
        jax.ShapeDtypeStruct((ROWS, D), BF),
        jax.ShapeDtypeStruct((64, 1536), F32),
        jax.ShapeDtypeStruct((64, 512), F32),
    )
    made = pl.pallas_call(
        kernel,
        out_shape=shapes,
        in_specs=[hbm, hbm, smem, hbm, hbm],
        out_specs=(hbm,) * 4,
        scratch_shapes=[
            pltpu.VMEM((ROWS, D), BF),
            pltpu.VMEM((ROWS, D), BF),
            pltpu.VMEM((64, 1536), F32),
            pltpu.VMEM((64, 512), F32),
            pltpu.VMEM((8, ROWS), F32),
            pltpu.VMEM((ROWS, D), BF),
            pltpu.VMEM((ROWS, D), BF),
            pltpu.VMEM((64, 1536), BF),
            pltpu.VMEM((64, 512), BF),
            pltpu.VMEM((2, 2, 64, 512), BF),
            pltpu.VMEM((2, D, 512), BF),
            pltpu.VMEM((ROWS, D), BF),
            pltpu.VMEM((ROWS, D), BF),
            pltpu.VMEM((8, ROWS), F32),
            pltpu.VMEM((2 * ROWS, D), BF),
            pltpu.VMEM((D, 2 * ROWS), BF),
            pltpu.VMEM((D, 2 * ROWS), BF),
            pltpu.VMEM((2 * ROWS, 128), F32),
            pltpu.VMEM((2 * ROWS, 384), BF),
            pltpu.VMEM((2 * ROWS, 128), BF),
            pltpu.VMEM((2, 2 * ROWS, 128), BF),
            pltpu.VMEM((2, 2 * ROWS, 384), BF),
            pltpu.VMEM((4, TILE, 2 * TILE), F32),
            pltpu.VMEM((2, 4, 4, 4, 64, 128), BF),
            pltpu.VMEM((2, 4, 3, 4, 64, 128), BF),
            pltpu.VMEM((2, 4, 4, 64, 128), BF),
            pltpu.VMEM((2, 4, 3, 64, 128), BF),
            pltpu.VMEM((2, 16, 16, 128), BF),
            pltpu.VMEM((2, NZ, 16, 128), BF),
            pltpu.VMEM((2, 16, 128), BF),
            pltpu.VMEM((2, 2, 16, 16, 128), BF),
            pltpu.VMEM((ROWS, D), BF),
            pltpu.VMEM((ROWS, D), BF),
            pltpu.VMEM((ROWS, D), BF),
            pltpu.VMEM((ROWS, D), BF),
            pltpu.VMEM((ROWS, D), F32),
            dma((4,)),
            dma((7,)),
            pltpu.SemaphoreType.REGULAR((3,)),
            dma((2, N_G)), dma((2, N_G)),
            dma((2, N_G)), dma((2, N_G)),
            dma((2,)), dma((2,)),
            dma((5,)), dma((5,)),
            dma((2, 4, 3)), dma((2, 4, 3)),
            dma((2, 4, 3)), dma((2, 4, 3)),
            dma((2, 2, 8)), dma((2,)),
            dma((2, NZ, 2)), dma((2,)),
        ],
        compiler_params=pltpu.CompilerParams(collective_id=0, has_side_effects=True, vmem_limit_bytes=62 * 2**20),
        name="layer",
    )(tokens, cotangent, lengths, input_weight, output_weight)
    return pl.pallas_call(
        hand_over,
        out_shape=shapes,
        in_specs=[hbm] * 4,
        out_specs=(hbm,) * 4,
        scratch_shapes=[pltpu.VMEM(leaf.shape, leaf.dtype) for leaf in shapes] + [dma((2, 4, 4))],
        compiler_params=pltpu.CompilerParams(vmem_limit_bytes=62 * 2**20),
        name="hand_over",
    )(*made)


def solution(mesh):
    placed = (
        P(("dp", "blk"), None),
        P(("dp", "blk")),
        P(("dp", "blk"), None),
        P("blk", None),
        P("blk", None),
    )
    return jax.shard_map(
        per_device,
        mesh=mesh,
        in_specs=placed,
        out_specs=(P(("dp", "blk"), None), P(("dp", "blk"), None), P("blk", None), P("blk", None)),
        check_vma=False,
    )
```
